512 devices in a mesh: tm: 64 (over x, z, core), rows: 8 (over y).
Axes of the slice: x: 4, y: 8, z: 8, core: 2. Of those that a mesh axis runs over, the one named last changes fastest.
Arguments:
- observations: float32 [128, 64, 1024], P('tm', 'rows'), may hold values from -6 to 6
- obs_noise: float32 [128, 64, 1024], P('tm', 'rows'), may hold values from -6 to 6
- prior_noise: float32 [128, 64, 1024], P('tm', 'rows'), may hold values from -4.8 to 4.8
- observed: int32 [128, 64, 1024], P('tm', 'rows'), may hold values 0 or 1
- kappa_sq: float32 [64, 1024], P('rows'), may hold values from 0.5 to 8
- obs_precision: float32 [64, 1024], P('rows'), may hold values from 0.2 to 2
Outputs:
- solution: float32 [128, 64, 1024], P('tm', 'rows')
- residual: float32 [128, 64, 1024], P('tm', 'rows')
- precond: float32 [128, 64, 1024], P('tm', 'rows')
The draws below stay inside these ranges and needn't reach their ends.
All inputs are finite; a program needn't handle non-finite values. No bound on the sum of `observed` on one device may be relied on, other than what follows from the above.
Results may differ from the reference program's by a relative error of at most 0.002.
Values sent between devices are 32-bit elements; how exact they have to be, the bound alone decides.
A program may use at most 64 MiB of HBM per device.

```python
import math
import jax
import jax.numpy as jnp
from jax import lax

COLS = 1024
ITERS = 2
HOURS = 128
ROWS = 64


def draw_prior_noise(key, part):
    hour_share = jnp.arange(HOURS, dtype=jnp.float32) / float(max(HOURS - 1, 1))
    amplitude = 0.1 + 1.1 * hour_share
    base_values = jnp.clip(jax.random.normal(key, (HOURS, ROWS, COLS), jnp.float32), -4.0, 4.0)
    return (base_values * amplitude[:, None, None]).astype(jnp.float32)


def place_ends(entries, key, low, largest):
    longest = entries.shape.index(max(entries.shape))
    spots = []
    for shift in (0, 1):
        where = [jax.random.randint(jax.random.fold_in(key, axis), (), 0, length) for axis, length in enumerate(entries.shape)]
        where[longest] = (where[longest] + shift) % entries.shape[longest]
        spots.append(tuple(where))
    return entries.at[spots[0]].set(low).at[spots[1]].set(largest)


def steps_of(key, shape, cuts, smallest, top_value):
    def one(position, blocks):
        draws = jax.random.uniform(jax.random.fold_in(jax.random.fold_in(key, 6), position), (blocks,), jnp.float32, smallest / len(cuts), top_value / len(cuts))
        return jnp.repeat(jnp.exp(draws), shape[position] // blocks).reshape((-1,) + (1,) * (len(shape) - position - 1))

    level = one(*cuts[0])
    for cut in cuts[1:]:
        level = level * one(*cut)
    return level


def normal_values(stream_key, shape, spread, bound, cuts=(), kind=jnp.bfloat16):
    array = jax.random.normal(stream_key, shape, jnp.float32) * spread
    if len(cuts) > 0:
        array = steps_of(stream_key, shape, cuts, -0.22, 0.18) * array
    return jnp.clip(array, min=-bound, max=bound).astype(kind)


def setup_inputs(seed: int = 0) -> dict:
    seeds = jax.random.split(jax.random.key(seed), 7)
    return {
        "observations": normal_values(seeds[0], (HOURS, ROWS, COLS), 1.0, 6.0, ((0, 64), (1, 8)), jnp.float32),
        "obs_noise": normal_values(seeds[1], (HOURS, ROWS, COLS), 1.0, 6.0, ((0, 64), (1, 8)), jnp.float32),
        "prior_noise": draw_prior_noise(jax.random.fold_in(seeds[6], 71), 0),
        "observed": place_ends((jax.random.randint(seeds[3], (HOURS, ROWS, COLS), 0, 4) < 1).astype(jnp.int32), jax.random.fold_in(seeds[3], 1), 0, 1),
        "kappa_sq": jnp.clip(jnp.exp(math.log(8.0) - 2.7725887 * jax.random.uniform(seeds[4], (ROWS, COLS), jnp.float32) ** steps_of(seeds[4], (ROWS, COLS), ((0, 8),), -0.2, 0.2)), 0.5, 8.0),
        "obs_precision": jnp.clip(jnp.exp(math.log(2.0) - 2.3025851 * jax.random.uniform(seeds[5], (ROWS, COLS), jnp.float32) ** steps_of(seeds[5], (ROWS, COLS), ((0, 8),), -0.2, 0.2)), 0.2, 2.0),
    }


coupling = 0.995

def hour_weights(count):
    inner = jnp.full((count,), 1.0 + coupling * coupling, jnp.float32)
    return inner.at[0].set(1.0).at[count - 1].set(1.0)

def operate(field, stencil_diag, weights, obs_weight):
    padded = jnp.pad(field, ((0, 0), (1, 1), (1, 1)))
    beside = padded[:, 2:, 1:-1] + padded[:, :-2, 1:-1] + padded[:, 1:-1, 2:] + padded[:, 1:-1, :-2]
    spatial = stencil_diag * field - beside
    hour_pad = jnp.pad(spatial, ((1, 1), (0, 0), (0, 0)))
    return weights * spatial - coupling * (hour_pad[2:] + hour_pad[:-2]) + obs_weight * field

def solve_hours(right_hand_part, main_diagonal_entries, offdiagonal_entries):

    def downward_solve(current_state, matrix_entries):
        previous_ratio, previous_elimination = current_state
        forcing_row, main_row = matrix_entries
        pivot_entry = main_row - offdiagonal_entries * previous_ratio
        current_ratio = offdiagonal_entries / pivot_entry
        current_elimination = (forcing_row - offdiagonal_entries * previous_elimination) / pivot_entry
        return ((current_ratio, current_elimination), (current_ratio, current_elimination))
    empty_field_grid = jnp.zeros_like(offdiagonal_entries)
    unused_item, (multiplier_list, elimination_list) = lax.scan(downward_solve, (empty_field_grid, empty_field_grid), (right_hand_part, main_diagonal_entries))

    def upward_solve(following_value, matrix_entries):
        multiplier_row, elimination_row = matrix_entries
        current_value = elimination_row - multiplier_row * following_value
        return (current_value, current_value)
    unused_item, value_list = lax.scan(upward_solve, empty_field_grid, (multiplier_list, elimination_list), reverse=True)
    return value_list

def reference(observations, obs_noise, prior_noise, observed, kappa_sq, obs_precision):
    maskf = observed.astype(jnp.float32)
    obs_weight = maskf * obs_precision
    right = maskf * (obs_precision * observations + jnp.sqrt(obs_precision) * obs_noise) + prior_noise
    stencil_diag = kappa_sq + 4.0
    weights = hour_weights(HOURS)[:, None, None]
    main_diagonal_entries = weights * stencil_diag + obs_weight
    offdiagonal_entries = -coupling * stencil_diag
    solution = jnp.zeros_like(right)
    residual = right
    precond = solve_hours(residual, main_diagonal_entries, offdiagonal_entries)
    direction = precond
    aligned = jnp.sum(residual * precond)
    for iteration in range(ITERS):
        applied = operate(direction, stencil_diag, weights, obs_weight)
        step_size = aligned / jnp.sum(direction * applied)
        solution = solution + step_size * direction
        residual = residual - step_size * applied
        precond = solve_hours(residual, main_diagonal_entries, offdiagonal_entries)
        aligned_new = jnp.sum(residual * precond)
        direction = precond + aligned_new / aligned * direction
        aligned = aligned_new
    return (solution, residual, precond)
```

```python
import jax
import jax.numpy as jnp
from jax import lax
from jax.experimental import pallas as pl
from jax.experimental.pallas import tpu as pltpu
from jax.sharding import PartitionSpec as P

RHO = 0.995
RHO_SQ = RHO * RHO
MESH = pl.DeviceIdType.MESH
F32 = jnp.float32
NT = 64
NY = 8
LEVELS = 7


def patch_of(m):
    x, z, c = m // 16, (m // 2) % 8, m % 2
    odd = x % 2
    return 16 * x + 2 * (z + odd * (7 - 2 * z)) + c


def device_of(j):
    return patch_of(j)


def iota(shape, axis):
    return lax.broadcasted_iota(jnp.int32, shape, axis)


def swap_blocks(v):
    shape, sub, lane = v.shape, v.ndim - 2, v.ndim - 1
    s, g = iota(shape, sub), iota(shape, lane) // 16
    for b in (1, 2, 4):
        down = pltpu.roll(pltpu.roll(v, 8 - b, sub), 16 * b, lane)
        s_b, g_b = (s // b) % 2, (g // b) % 2
        if b == 4:
            v = jnp.where(s_b == g_b, v, down)
        else:
            up = pltpu.roll(pltpu.roll(v, b, sub), 128 - 16 * b, lane)
            v = jnp.where(s_b == g_b, v, jnp.where(s_b == 0, down, up))
    return v


def lane_sum(v):
    return jnp.sum(v, axis=1, keepdims=True)


def fold(v):
    return jnp.sum(v.reshape(v.shape[0] // 8, 8, 128), axis=0)


def kernel(
    obs_ref, noise_ref, prior_ref, mask_ref, kappa_ref, prec_ref,
    x_ref, r_ref, p_ref,
    s_mask, s_right, b_mask, b_right, stencil, omega, gain, last, rc, nc,
    s_z, s_one, s_two, b_z, b_one, b_two, pads, cols_out, side_in, rows_in,
    sums_y, sums_t, mine, one_row,
    send_big, recv_big, halo_send, halo_recv, sum_send, sum_recv, own_sem,
):
    me, y = lax.axis_index("tm"), lax.axis_index("rows")
    j = patch_of(me)

    barrier = pltpu.get_barrier_semaphore()

    def greet(k, carry):
        t = lax.rem(me + k, NT)
        pl.semaphore_signal(barrier, inc=1, device_id={"tm": t}, device_id_type=MESH)
        return carry

    lax.fori_loop(1, NT, greet, 0)

    def greet_rows(k, carry):
        t = lax.rem(y + k, NY)
        pl.semaphore_signal(barrier, inc=1, device_id={"rows": t}, device_id_type=MESH)
        return carry

    lax.fori_loop(1, NY, greet_rows, 0)

    for tile in range(8):
        cols = slice(128 * tile, 128 * tile + 128)
        mask = mask_ref[:, :, cols].astype(F32)
        prec = prec_ref[:, cols][None]
        right = mask * (prec * obs_ref[:, :, cols] + jnp.sqrt(prec) * noise_ref[:, :, cols])
        right = right + prior_ref[:, :, cols]
        r_ref[:, :, cols] = right
        mask, right = swap_blocks(mask), swap_blocks(right)
        for h in range(2):
            s_mask[pl.ds(16 * tile + h, 8, stride=2), :] = mask[h]
            s_right[pl.ds(16 * tile + h, 8, stride=2), :] = right[h]

    pl.semaphore_wait(barrier, NT - 1 + NY - 1)

    def to_patches(src, dst, slot):
        def send(i, carry):
            t = lax.rem(me + 1 + lax.rem(i + 23, NT - 1), NT)
            pltpu.make_async_remote_copy(
                src_ref=src.at[pl.ds(2 * patch_of(t), 2)],
                dst_ref=dst.at[pl.ds(2 * me, 2)],
                send_sem=send_big.at[slot],
                recv_sem=recv_big.at[slot],
                device_id={"tm": t},
                device_id_type=MESH,
            ).start()
            return carry

        lax.fori_loop(0, NT - 1, send, 0)
        own = pltpu.make_async_copy(
            src.at[pl.ds(2 * j, 2)], dst.at[pl.ds(2 * me, 2)], own_sem.at[slot]
        )
        own.start()
        return own

    def to_hours(src, dst, slot, rows):
        def send(i, carry):
            t = lax.rem(me + 1 + lax.rem(i + 23, NT - 1), NT)
            pltpu.make_async_remote_copy(
                src_ref=src.at[pl.ds(rows * t, rows)],
                dst_ref=dst.at[pl.ds(rows * j, rows)],
                send_sem=send_big.at[slot],
                recv_sem=recv_big.at[slot],
                device_id={"tm": t},
                device_id_type=MESH,
            ).start()
            return carry

        lax.fori_loop(0, NT - 1, send, 0)
        own = pltpu.make_async_copy(
            src.at[pl.ds(rows * me, rows)], dst.at[pl.ds(rows * j, rows)], own_sem.at[slot]
        )
        own.start()
        return own

    def big(src, dst, slot, rows):
        n = rows * (NT - 1)
        return pltpu.make_async_remote_copy(
            src_ref=src.at[pl.ds(0, n)],
            dst_ref=dst.at[pl.ds(0, n)],
            send_sem=send_big.at[slot],
            recv_sem=recv_big.at[slot],
            device_id={"tm": lax.rem(me + 1, NT)},
            device_id_type=MESH,
        )

    own_mask = to_patches(s_mask, b_mask, 0)
    own_right = to_patches(s_right, b_right, 1)

    tile, back = j // 8, j % 8
    shift = lax.rem(128 - 16 * back, 128)
    columns = pl.ds(pl.multiple_of(tile * 128, 128), 128)

    def per_cell(ref):
        rows = pltpu.roll(ref[:, columns], shift, 1)
        turned = jnp.concatenate([rows, jnp.zeros((120, 128), F32)], axis=0).T
        return [jnp.broadcast_to(turned[0:16, r : r + 1], (16, 128)) for r in range(8)]

    kappa, prec = per_cell(kappa_ref), per_cell(prec_ref)
    for r in range(8):
        diag = 1.0 / (kappa[r] + 4.0)
        stencil[pl.ds(16 * r, 16), :] = diag
        omega[pl.ds(16 * r, 16), :] = prec[r] * diag

    own_mask.wait()
    big(s_mask, b_mask, 0, 2).wait_recv()
    omega[...] = omega[...] * b_mask[...].T

    def factor(i, carry):
        at = pl.ds(pl.multiple_of(32 * i, 32), 32)
        lane = iota((32, 128), 1)
        w = omega[at, :]
        first = lane == 0
        a = jnp.where(first, 0.0, w + RHO_SQ)
        b = w
        c = jnp.where(first, 0.0, 1.0)
        d = jnp.ones_like(w)
        for k in range(LEVELS):
            s = 1 << k
            keep = lane < s
            pb, pd = pltpu.roll(b, s, 1), pltpu.roll(d, s, 1)
            nb, nd = a * pb + b * pd, c * pb + d * pd
            if k < LEVELS - 1:
                pa, pc = pltpu.roll(a, s, 1), pltpu.roll(c, s, 1)
                na, nc_ = a * pa + b * pc, c * pa + d * pc
                a, c = jnp.where(keep, a, na), jnp.where(keep, c, nc_)
            b, d = jnp.where(keep, b, nb), jnp.where(keep, d, nd)
            if k == LEVELS - 2:
                scale = 1.0 / (c + d)
                a, b, c, d = a * scale, b * scale, c * scale, d * scale
        sigma = b / d
        before = pltpu.roll(sigma, 1, 1)
        final = lane == 127
        pivot = jnp.where(final, w + ((1.0 - RHO_SQ) + before) / (1.0 + before), 1.0 + sigma)
        inverse = 1.0 / pivot
        last[at, :] = inverse
        g = pltpu.roll(jnp.where(final, 0.0, RHO * inverse), 1, 1)
        for k in range(LEVELS):
            gain[k, at, :] = g
            if k < LEVELS - 1:
                g = g * pltpu.roll(g, 1 << k, 1)
        return carry

    lax.fori_loop(0, 4, factor, 0)

    def solve(v):
        v = v * stencil[...]
        for k in range(LEVELS):
            v = v + gain[k] * pltpu.roll(v, 1 << k, 1)
        v = v * last[...]
        for k in range(LEVELS):
            v = v + pltpu.roll(gain[k] * v, 128 - (1 << k), 1)
        return v

    left, right_dev = device_of(lax.rem(j + NT - 1, NT)), device_of(lax.rem(j + 1, NT))
    above, below = lax.rem(y + NY - 1, NY), lax.rem(y + 1, NY)

    def halo_copies(n):
        pad = pads.at[n]
        parts = (
            (pad.at[pl.ds(8, 16)], rows_in.at[n, 1], {"rows": above}),
            (pad.at[pl.ds(32 * 7 + 8, 16)], rows_in.at[n, 0], {"rows": below}),
            (cols_out.at[n, 0], side_in.at[n, 1], {"tm": left}),
            (cols_out.at[n, 1], side_in.at[n, 0], {"tm": right_dev}),
        )
        return [
            pltpu.make_async_remote_copy(
                src_ref=src,
                dst_ref=dst,
                send_sem=halo_send.at[4 * n + i],
                recv_sem=halo_recv.at[4 * n + i],
                device_id=to,
                device_id_type=MESH,
            )
            for i, (src, dst, to) in enumerate(parts)
        ]

    def halo_start(n, v):
        for r in range(8):
            pads[n, pl.ds(32 * r + 8, 16), :] = v[16 * r : 16 * r + 16]
        cols_out[n, 0] = pads[n, pl.ds(8, 8, stride=32), :]
        cols_out[n, 1] = pads[n, pl.ds(23, 8, stride=32), :]
        copies = halo_copies(n)
        for copy in copies:
            copy.start()
        return copies

    hour = iota((16, 128), 1)
    from_before = jnp.where(hour == 0, 0.0, RHO).astype(F32)
    from_after = jnp.where(hour == 127, 0.0, RHO).astype(F32)
    weight = jnp.where((hour == 0) | (hour == 127), 1.0, 1.0 + RHO_SQ).astype(F32)

    def neighbours(n, copies):
        for copy in copies:
            copy.wait_recv()
        pads[n, pl.ds(7, 8, stride=32), :] = jnp.where(j == 0, 0.0, side_in[n, 0])
        pads[n, pl.ds(24, 8, stride=32), :] = jnp.where(j == NT - 1, 0.0, side_in[n, 1])
        for r in range(8):
            if r == 0:
                up = jnp.where(y == 0, 0.0, rows_in[n, 0])
            else:
                up = pads[n, pl.ds(32 * (r - 1) + 8, 16), :]
            if r == 7:
                down = jnp.where(y == NY - 1, 0.0, rows_in[n, 1])
            else:
                down = pads[n, pl.ds(32 * (r + 1) + 8, 16), :]
            u = pads[n, pl.ds(32 * r + 7, 16), :] + pads[n, pl.ds(32 * r + 9, 16), :]
            u = u + (up + down)
            u = weight * u - (
                from_before * pltpu.roll(u, 1, 1) + from_after * pltpu.roll(u, 127, 1)
            )
            nc[pl.ds(16 * r, 16), :] = u
        return nc[...]

    own_right.wait()
    big(s_right, b_right, 1, 2).wait_recv()
    rc[...] = b_right[...].T
    z0 = solve(rc[...])
    copies_0 = halo_start(0, z0)
    s_z[...] = z0.T
    own_z = to_hours(s_z, b_z, 2, 2)
    rz_part = fold(rc[...] * z0)

    n0 = neighbours(0, copies_0)
    s0 = solve(n0)
    copies_1 = halo_start(1, s0)

    def interleave(ref, even, odd):
        ref[pl.ds(0, 128, stride=2), :] = even.T
        ref[pl.ds(1, 128, stride=2), :] = odd.T

    interleave(s_one, n0, s0)
    own_one = to_hours(s_one, b_one, 3, 4)
    e1_part = fold(rc[...] * s0)
    e2_part = fold(n0 * s0)

    n1 = neighbours(1, copies_1)
    e3_part = fold(n1 * jnp.concatenate([pads[1, pl.ds(32 * r + 8, 16), :] for r in range(8)], axis=0))

    sub = iota((8, 128), 0)
    total = jnp.zeros((8, 128), F32)
    for i, part in enumerate((rz_part, e1_part, e2_part, e3_part)):
        total = jnp.where(sub == i, jnp.sum(part, axis=0, keepdims=True), total)
    mine[...] = total
    sums_y[pl.ds(pl.multiple_of(8 * y, 8), 8), :] = total

    def rows_copy(t):
        return pltpu.make_async_remote_copy(
            src_ref=mine,
            dst_ref=sums_y.at[pl.ds(pl.multiple_of(8 * y, 8), 8)],
            send_sem=sum_send.at[0],
            recv_sem=sum_recv.at[0],
            device_id={"rows": t},
            device_id_type=MESH,
        )

    def send_rows(k, carry):
        rows_copy(lax.rem(y + k, NY)).start()
        return carry

    lax.fori_loop(1, NY, send_rows, 0)

    s1 = solve(n1)
    interleave(s_two, n1, s1)
    own_two = to_hours(s_two, b_two, 4, 4)

    def all_rows(n, src, dst, slot):
        return pltpu.make_async_remote_copy(
            src_ref=src.at[pl.ds(0, n)],
            dst_ref=dst.at[pl.ds(0, n)],
            send_sem=sum_send.at[slot],
            recv_sem=sum_recv.at[slot],
            device_id={"rows": lax.rem(y + 1, NY)},
            device_id_type=MESH,
        )

    all_rows(8 * (NY - 1), sums_y, sums_y, 0).wait_recv()
    part = fold(sums_y[...])
    part = part + pltpu.roll(part, 64, 1)
    part = part + pltpu.roll(part, 32, 1)
    part = jnp.where(iota((8, 128), 1) // 32 == sub, part, 0.0)
    one_row[...] = jnp.broadcast_to(jnp.sum(part, axis=0, keepdims=True), (8, 128))
    sums_t[pl.ds(me, 1), :] = one_row[0:1, :]

    def send_sums(i, carry):
        t = lax.rem(me + 1 + lax.rem(i + 23, NT - 1), NT)
        pltpu.make_async_remote_copy(
            src_ref=one_row.at[pl.ds(0, 1)],
            dst_ref=sums_t.at[pl.ds(me, 1)],
            send_sem=sum_send.at[1],
            recv_sem=sum_recv.at[1],
            device_id={"tm": t},
            device_id_type=MESH,
        ).start()
        return carry

    lax.fori_loop(0, NT - 1, send_sums, 0)

    own_z.wait()
    big(s_z, b_z, 2, 2).wait_recv()
    own_one.wait()
    big(s_one, b_one, 3, 4).wait_recv()
    own_two.wait()
    big(s_two, b_two, 4, 4).wait_recv()
    for ref, stride in ((b_z, 2), (b_one, 4), (b_two, 4)):
        for tile in range(8):
            for o in range(stride):
                at = pl.ds(8 * stride * tile + o, 8, stride=stride)
                ref[at, :] = swap_blocks(ref[at, :])

    all_rows(NT - 1, sums_t, sums_t, 1).wait_recv()
    sums = jnp.sum(fold(sums_t[...]), axis=0, keepdims=True)
    group = iota((1, 128), 1) // 32
    rz0, e1, e2, e3 = [lane_sum(jnp.where(group == i, sums, 0.0)) for i in range(4)]
    curved = rz0 - e1
    alpha0 = rz0 / curved
    beta0 = (e2 * rz0 - e1 * e1) / (curved * curved)
    along = 1.0 + beta0 - alpha0
    curved1 = along * along * curved + 2.0 * along * alpha0 * (e1 - e2) + alpha0 * alpha0 * (e2 - e3)
    alpha1 = beta0 * rz0 / curved1
    first = alpha0 + alpha1 * (1.0 + beta0)
    second = alpha0 * alpha1
    c0, c1 = 1.0 - first + second, first - 2.0 * second

    for tile in range(8):
        cols = slice(128 * tile, 128 * tile + 128)
        for h in range(2):
            z = b_z[pl.ds(16 * tile + h, 8, stride=2), :]
            n_a = b_one[pl.ds(32 * tile + 2 * h, 8, stride=4), :]
            s_a = b_one[pl.ds(32 * tile + 2 * h + 1, 8, stride=4), :]
            n_b = b_two[pl.ds(32 * tile + 2 * h, 8, stride=4), :]
            s_b = b_two[pl.ds(32 * tile + 2 * h + 1, 8, stride=4), :]
            x_ref[h, :, cols] = (first - second) * z + second * s_a
            r_ref[h, :, cols] = c0 * r_ref[h, :, cols] + c1 * n_a + second * n_b
            p_ref[h, :, cols] = c0 * z + c1 * s_a + second * s_b

    for copy in copies_0 + copies_1:
        copy.wait_send()
    big(s_mask, b_mask, 0, 2).wait_send()
    big(s_right, b_right, 1, 2).wait_send()
    big(s_z, b_z, 2, 2).wait_send()
    big(s_one, b_one, 3, 4).wait_send()
    big(s_two, b_two, 4, 4).wait_send()
    all_rows(8 * (NY - 1), sums_y, sums_y, 0).wait_send()
    all_rows(NT - 1, sums_t, sums_t, 1).wait_send()


def per_device(observations, obs_noise, prior_noise, observed, kappa_sq, obs_precision):
    vmem = pl.BlockSpec(memory_space=pltpu.VMEM)
    out = jax.ShapeDtypeStruct(observations.shape, F32)

    def buf(*shape):
        return pltpu.VMEM(shape, F32)

    return pl.pallas_call(
        kernel,
        out_shape=(out, out, out),
        in_specs=[vmem] * 6,
        out_specs=(vmem,) * 3,
        scratch_shapes=[
            buf(128, 128), buf(128, 128), buf(128, 128), buf(128, 128),
            buf(128, 128), buf(128, 128), buf(LEVELS, 128, 128), buf(128, 128),
            buf(128, 128), buf(128, 128),
            buf(128, 128), buf(256, 128), buf(256, 128),
            buf(128, 128), buf(256, 128), buf(256, 128),
            buf(2, 256, 128), buf(2, 2, 8, 128), buf(2, 2, 8, 128), buf(2, 2, 16, 128),
            buf(64, 128), buf(64, 128), buf(8, 128), buf(8, 128),
            pltpu.SemaphoreType.DMA((5,)), pltpu.SemaphoreType.DMA((5,)),
            pltpu.SemaphoreType.DMA((8,)), pltpu.SemaphoreType.DMA((8,)),
            pltpu.SemaphoreType.DMA((2,)), pltpu.SemaphoreType.DMA((2,)),
            pltpu.SemaphoreType.DMA((5,)),
        ],
        compiler_params=pltpu.CompilerParams(collective_id=0, has_side_effects=True),
    )(observations, obs_noise, prior_noise, observed, kappa_sq, obs_precision)


def solution(mesh):
    in_specs = (P("tm", "rows", None),) * 4 + (P("rows", None),) * 2
    out_specs = (P("tm", "rows", None),) * 3
    return jax.shard_map(
        per_device, mesh=mesh, in_specs=in_specs, out_specs=out_specs, check_vma=False
    )
```

```python
import jax
import jax.numpy as jnp
from jax import lax
from jax.experimental import pallas as pl
from jax.experimental.pallas import tpu as pltpu
from jax.sharding import PartitionSpec as P

RHO = 0.995
RHO_SQ = RHO * RHO
MESH = pl.DeviceIdType.MESH
F32 = jnp.float32
NT = 64
NY = 8
LEVELS = 7


def patch_of(m):
    x, z, c = m // 16, (m // 2) % 8, m % 2
    odd = x % 2
    return 16 * x + 2 * (z + odd * (7 - 2 * z)) + c


def device_of(j):
    return patch_of(j)


def ring_tile(tile):
    return tile + (0, 0, 1, -1)[tile % 4]


def ring_order(v, tile):
    if tile % 4 < 2:
        return v
    axis = v.ndim - 2
    v = pltpu.roll(v, 4, axis)
    even = (iota(v.shape, axis) // 2) % 2 == 0
    return jnp.where(even, pltpu.roll(v, 6, axis), pltpu.roll(v, 2, axis))


def iota(shape, axis):
    return lax.broadcasted_iota(jnp.int32, shape, axis)


def swap_blocks(v):
    shape, sub, lane = v.shape, v.ndim - 2, v.ndim - 1
    s, g = iota(shape, sub), iota(shape, lane) // 16
    for b in (1, 2, 4):
        down = pltpu.roll(pltpu.roll(v, 8 - b, sub), 16 * b, lane)
        s_b, g_b = (s // b) % 2, (g // b) % 2
        if b == 4:
            v = jnp.where(s_b == g_b, v, down)
        else:
            up = pltpu.roll(pltpu.roll(v, b, sub), 128 - 16 * b, lane)
            v = jnp.where(s_b == g_b, v, jnp.where(s_b == 0, down, up))
    return v


def lane_sum(v):
    return jnp.sum(v, axis=1, keepdims=True)


def fold(v):
    return jnp.sum(v.reshape(v.shape[0] // 8, 8, 128), axis=0)


def kernel(
    obs_hbm, noise_hbm, prior_hbm, mask_hbm, kappa_hbm, prec_hbm,
    z_hbm, na_hbm, sa_hbm, nb_hbm, sb_hbm, r_hbm, coef_ref,
    obs_ref, noise_ref, prior_ref, mask_ref, kappa_ref, prec_ref,
    z_all, na_all, sa_all, nb_all, sb_all, r_all,
    s_mask, s_right, b_mask, b_right, stencil, gain, last, rc, nc,
    s_z, s_one, s_two, b_z, b_one, b_two, pads, cols_out, side_in, rows_in,
    sums_y, sums_t, mine, one_row,
    send_big, recv_big, halo_send, halo_recv, sum_send, sum_recv, own_sem, in_sem, out_sem,
):
    me, y = lax.axis_index("tm"), lax.axis_index("rows")
    j = patch_of(me)

    barrier = pltpu.get_barrier_semaphore()

    def each_peer(act):
        def block(b, carry):
            base = me + 22 + 7 * b + jnp.where(b >= 6, 1, 0)
            base = base - jnp.where(base >= NT, NT, 0)
            base = base - jnp.where(base >= NT, NT, 0)
            for i in range(7):
                t = base + i
                act(t - jnp.where(t >= NT, NT, 0))
            return carry

        lax.fori_loop(0, 9, block, 0)

    def greet(t):
        pl.semaphore_signal(barrier, inc=1, device_id={"tm": t}, device_id_type=MESH)

    each_peer(greet)
    for k in range(1, NY):
        t = lax.rem(y + k, NY)
        pl.semaphore_signal(barrier, inc=1, device_id={"rows": t}, device_id_type=MESH)

    loads = [
        pltpu.make_async_copy(src, dst, in_sem.at[i])
        for i, (src, dst) in enumerate(
            (
                (mask_hbm, mask_ref),
                (obs_hbm, obs_ref),
                (noise_hbm, noise_ref),
                (prior_hbm, prior_ref),
                (prec_hbm, prec_ref),
                (kappa_hbm, kappa_ref),
            )
        )
    ]
    for load in loads:
        load.start()
    for load in loads:
        load.wait()

    for tile in range(8):
        cols = slice(128 * tile, 128 * tile + 128)
        mask = mask_ref[:, :, cols].astype(F32)
        prec = prec_ref[:, cols][None]
        right = mask * (prec * obs_ref[:, :, cols] + jnp.sqrt(prec) * noise_ref[:, :, cols])
        right = right + prior_ref[:, :, cols]
        r_all[:, :, cols] = right
        mask, right = ring_order(swap_blocks(mask), tile), ring_order(swap_blocks(right), tile)
        for h in range(2):
            at = pl.ds(16 * ring_tile(tile) + h, 8, stride=2)
            s_mask[at, :] = mask[h]
            s_right[at, :] = right[h]

    pl.semaphore_wait(barrier, NT - 1 + NY - 1)

    def to_all(src, dst, slot, rows):
        def send(t):
            pltpu.make_async_remote_copy(
                src_ref=src.at[pl.ds(rows * t, rows)],
                dst_ref=dst.at[pl.ds(rows * me, rows)],
                send_sem=send_big.at[slot],
                recv_sem=recv_big.at[slot],
                device_id={"tm": t},
                device_id_type=MESH,
            ).start()

        each_peer(send)
        own = pltpu.make_async_copy(
            src.at[pl.ds(rows * me, rows)], dst.at[pl.ds(rows * me, rows)], own_sem.at[slot]
        )
        own.start()
        return own

    def big(src, dst, slot, rows):
        n = rows * (NT - 1)
        return pltpu.make_async_remote_copy(
            src_ref=src.at[pl.ds(0, n)],
            dst_ref=dst.at[pl.ds(0, n)],
            send_sem=send_big.at[slot],
            recv_sem=recv_big.at[slot],
            device_id={"tm": lax.rem(me + 1, NT)},
            device_id_type=MESH,
        )

    own_mask = to_all(s_mask, b_mask, 0, 2)
    own_right = to_all(s_right, b_right, 1, 2)

    tile, back = j // 8, j % 8
    shift = lax.rem(128 - 16 * back, 128)
    columns = pl.ds(pl.multiple_of(tile * 128, 128), 128)

    def per_cell(ref):
        rows = pltpu.roll(ref[:, columns], shift, 1)
        turned = jnp.concatenate([rows, jnp.zeros((120, 128), F32)], axis=0).T
        return [jnp.broadcast_to(turned[0:16, r : r + 1], (16, 128)) for r in range(8)]

    kappa = per_cell(kappa_ref)
    for r in range(8):
        stencil[pl.ds(16 * r, 16), :] = 1.0 / (kappa[r] + 4.0)
    one_row[...] = swap_blocks(prec_ref[:, columns] / (kappa_ref[:, columns] + 4.0))
    ratio = one_row[pl.ds(back, 1), :]

    own_mask.wait()
    big(s_mask, b_mask, 0, 2).wait_recv()

    seg = iota((8, 128), 0)
    ones, zeros = jnp.ones((8, 128), F32), jnp.zeros((8, 128), F32)
    w = [b_mask[pl.ds(k, 8, stride=16), :] * ratio for k in range(16)]
    a, b, c, d = ones, zeros, zeros, ones
    for k in range(16):
        ac, bd = a + c, b + d
        a, b, c, d = w[k] * ac + RHO_SQ * a, w[k] * bd + RHO_SQ * b, ac, bd
    scale = 1.0 / (c + d)
    a, b, c, d = a * scale, b * scale, c * scale, d * scale
    for n in (1, 2, 4):
        pa, pb, pc, pd = [pltpu.roll(q, n, 0) for q in (a, b, c, d)]
        keep = seg < n
        a, b, c, d = [
            jnp.where(keep, old, new)
            for old, new in zip(
                (a, b, c, d),
                (a * pa + b * pc, a * pb + b * pd, c * pa + d * pc, c * pb + d * pd),
            )
        ]
    b = jnp.where(seg == 0, 0.0, pltpu.roll(b, 1, 0))
    d = jnp.where(seg == 0, 1.0, pltpu.roll(d, 1, 0))
    for k in range(16):
        before_b, before_d = b, d
        bd = b + d
        b, d = w[k] * bd + RHO_SQ * b, bd
        pivot = (b + d) / d
        if k == 15:
            before = before_b / before_d
            final = w[k] + ((1.0 - RHO_SQ) + before) / (1.0 + before)
            pivot = jnp.where(seg == 7, final, pivot)
        rc[pl.ds(k, 8, stride=16), :] = 1.0 / pivot
    inverse = rc[...].T
    last[...] = inverse
    g = pltpu.roll(jnp.where(iota((128, 128), 1) == 127, 0.0, RHO * inverse), 1, 1)
    for k in range(LEVELS):
        gain[k] = g
        if k < LEVELS - 1:
            g = g * pltpu.roll(g, 1 << k, 1)

    def solve(v):
        v = v * stencil[...]
        for k in range(LEVELS):
            v = v + gain[k] * pltpu.roll(v, 1 << k, 1)
        v = v * last[...]
        for k in range(LEVELS):
            v = v + pltpu.roll(gain[k] * v, 128 - (1 << k), 1)
        return v

    left, right_dev = device_of(lax.rem(j + NT - 1, NT)), device_of(lax.rem(j + 1, NT))
    above, below = lax.rem(y + NY - 1, NY), lax.rem(y + 1, NY)

    def halo_copies(n):
        pad = pads.at[n]
        parts = (
            (pad.at[pl.ds(8, 16)], rows_in.at[n, 1], {"rows": above}),
            (pad.at[pl.ds(32 * 7 + 8, 16)], rows_in.at[n, 0], {"rows": below}),
            (cols_out.at[n, 0], side_in.at[n, 1], {"tm": left}),
            (cols_out.at[n, 1], side_in.at[n, 0], {"tm": right_dev}),
        )
        return [
            pltpu.make_async_remote_copy(
                src_ref=src,
                dst_ref=dst,
                send_sem=halo_send.at[4 * n + i],
                recv_sem=halo_recv.at[4 * n + i],
                device_id=to,
                device_id_type=MESH,
            )
            for i, (src, dst, to) in enumerate(parts)
        ]

    def halo_start(n, v):
        for r in range(8):
            pads[n, pl.ds(32 * r + 8, 16), :] = v[16 * r : 16 * r + 16]
        cols_out[n, 0] = pads[n, pl.ds(8, 8, stride=32), :]
        cols_out[n, 1] = pads[n, pl.ds(23, 8, stride=32), :]
        copies = halo_copies(n)
        for copy in copies:
            copy.start()
        return copies

    hour = iota((16, 128), 1)
    from_before = jnp.where(hour == 0, 0.0, RHO).astype(F32)
    from_after = jnp.where(hour == 127, 0.0, RHO).astype(F32)
    weight = jnp.where((hour == 0) | (hour == 127), 1.0, 1.0 + RHO_SQ).astype(F32)

    def neighbours(n, copies):
        for copy in copies:
            copy.wait_recv()
        pads[n, pl.ds(7, 8, stride=32), :] = jnp.where(j == 0, 0.0, side_in[n, 0])
        pads[n, pl.ds(24, 8, stride=32), :] = jnp.where(j == NT - 1, 0.0, side_in[n, 1])
        for r in range(8):
            if r == 0:
                up = jnp.where(y == 0, 0.0, rows_in[n, 0])
            else:
                up = pads[n, pl.ds(32 * (r - 1) + 8, 16), :]
            if r == 7:
                down = jnp.where(y == NY - 1, 0.0, rows_in[n, 1])
            else:
                down = pads[n, pl.ds(32 * (r + 1) + 8, 16), :]
            u = pads[n, pl.ds(32 * r + 7, 16), :] + pads[n, pl.ds(32 * r + 9, 16), :]
            u = u + (up + down)
            u = weight * u - (
                from_before * pltpu.roll(u, 1, 1) + from_after * pltpu.roll(u, 127, 1)
            )
            nc[pl.ds(16 * r, 16), :] = u
        return nc[...]

    own_right.wait()
    big(s_right, b_right, 1, 2).wait_recv()
    rc[...] = b_right[...].T
    z0 = solve(rc[...])
    copies_0 = halo_start(0, z0)
    s_z[...] = z0.T
    own_z = to_all(s_z, b_z, 2, 2)
    rz_part = fold(rc[...] * z0)

    n0 = neighbours(0, copies_0)
    s0 = solve(n0)
    copies_1 = halo_start(1, s0)

    def interleave(ref, even, odd):
        ref[pl.ds(0, 128, stride=2), :] = even.T
        ref[pl.ds(1, 128, stride=2), :] = odd.T

    interleave(s_one, n0, s0)
    own_one = to_all(s_one, b_one, 3, 4)
    e1_part = fold(rc[...] * s0)
    e2_part = fold(n0 * s0)

    n1 = neighbours(1, copies_1)
    e3_part = fold(n1 * jnp.concatenate([pads[1, pl.ds(32 * r + 8, 16), :] for r in range(8)], axis=0))

    sub = iota((8, 128), 0)
    total = jnp.zeros((8, 128), F32)
    for i, part in enumerate((rz_part, e1_part, e2_part, e3_part)):
        total = jnp.where(sub == i, jnp.sum(part, axis=0, keepdims=True), total)
    mine[...] = total
    sums_y[pl.ds(pl.multiple_of(8 * y, 8), 8), :] = total

    def rows_copy(t):
        return pltpu.make_async_remote_copy(
            src_ref=mine,
            dst_ref=sums_y.at[pl.ds(pl.multiple_of(8 * y, 8), 8)],
            send_sem=sum_send.at[0],
            recv_sem=sum_recv.at[0],
            device_id={"rows": t},
            device_id_type=MESH,
        )

    def send_rows(k, carry):
        rows_copy(lax.rem(y + k, NY)).start()
        return carry

    lax.fori_loop(1, NY, send_rows, 0)

    s1 = solve(n1)
    interleave(s_two, n1, s1)
    own_two = to_all(s_two, b_two, 4, 4)

    def all_rows(n, src, dst, slot):
        return pltpu.make_async_remote_copy(
            src_ref=src.at[pl.ds(0, n)],
            dst_ref=dst.at[pl.ds(0, n)],
            send_sem=sum_send.at[slot],
            recv_sem=sum_recv.at[slot],
            device_id={"rows": lax.rem(y + 1, NY)},
            device_id_type=MESH,
        )

    all_rows(8 * (NY - 1), sums_y, sums_y, 0).wait_recv()
    part = fold(sums_y[...])
    part = part + pltpu.roll(part, 64, 1)
    part = part + pltpu.roll(part, 32, 1)
    part = jnp.where(iota((8, 128), 1) // 32 == sub, part, 0.0)
    one_row[...] = jnp.broadcast_to(jnp.sum(part, axis=0, keepdims=True), (8, 128))
    sums_t[pl.ds(me, 1), :] = one_row[0:1, :]

    def send_sums(i, carry):
        t = lax.rem(me + 1 + lax.rem(i + 23, NT - 1), NT)
        pltpu.make_async_remote_copy(
            src_ref=one_row.at[pl.ds(0, 1)],
            dst_ref=sums_t.at[pl.ds(me, 1)],
            send_sem=sum_send.at[1],
            recv_sem=sum_recv.at[1],
            device_id={"tm": t},
            device_id_type=MESH,
        ).start()
        return carry

    lax.fori_loop(0, NT - 1, send_sums, 0)

    stores = []
    store = pltpu.make_async_copy(r_all, r_hbm, out_sem.at[5])
    store.start()
    stores.append(store)
    outs = (
        (0, b_z, 2, 0, z_all, z_hbm),
        (1, b_one, 4, 0, na_all, na_hbm),
        (2, b_one, 4, 1, sa_all, sa_hbm),
        (3, b_two, 4, 0, nb_all, nb_hbm),
        (4, b_two, 4, 1, sb_all, sb_hbm),
    )
    for i, ref, stride, o, dst, hbm in outs:
        if i == 0:
            own_z.wait()
            big(s_z, b_z, 2, 2).wait_recv()
        elif i == 1:
            own_one.wait()
            big(s_one, b_one, 3, 4).wait_recv()
        elif i == 3:
            own_two.wait()
            big(s_two, b_two, 4, 4).wait_recv()
        for tile in range(8):
            for h in range(2):
                at = pl.ds(8 * stride * ring_tile(tile) + h * (stride // 2) + o, 8, stride=stride)
                dst[h, :, 128 * tile : 128 * tile + 128] = swap_blocks(ring_order(ref[at, :], tile))
        store = pltpu.make_async_copy(dst, hbm, out_sem.at[i])
        store.start()
        stores.append(store)

    all_rows(NT - 1, sums_t, sums_t, 1).wait_recv()
    sums = jnp.sum(fold(sums_t[...]), axis=0, keepdims=True)
    group = iota((1, 128), 1) // 32
    rz0, e1, e2, e3 = [lane_sum(jnp.where(group == i, sums, 0.0)) for i in range(4)]
    curved = rz0 - e1
    alpha0 = rz0 / curved
    beta0 = (e2 * rz0 - e1 * e1) / (curved * curved)
    along = 1.0 + beta0 - alpha0
    curved1 = along * along * curved + 2.0 * along * alpha0 * (e1 - e2) + alpha0 * alpha0 * (e2 - e3)
    alpha1 = beta0 * rz0 / curved1
    first = alpha0 + alpha1 * (1.0 + beta0)
    second = alpha0 * alpha1
    c0, c1 = 1.0 - first + second, first - 2.0 * second

    row = iota((8, 128), 0)
    coef_ref[...] = jnp.where(
        row == 0,
        first - second,
        jnp.where(row == 1, second, jnp.where(row == 2, c0, c1)),
    )
    for store in stores:
        store.wait()
    for copy in copies_0 + copies_1:
        copy.wait_send()
    big(s_mask, b_mask, 0, 2).wait_send()
    big(s_right, b_right, 1, 2).wait_send()
    big(s_z, b_z, 2, 2).wait_send()
    big(s_one, b_one, 3, 4).wait_send()
    big(s_two, b_two, 4, 4).wait_send()
    all_rows(8 * (NY - 1), sums_y, sums_y, 0).wait_send()
    all_rows(NT - 1, sums_t, sums_t, 1).wait_send()


def combine(z_ref, na_ref, sa_ref, nb_ref, sb_ref, r_ref, coef_ref, x_out, r_out, p_out):
    q0, q1, q2, q3 = [coef_ref[i : i + 1, 0:1].reshape(1, 1, 1) for i in range(4)]
    for tile in range(8):
        at = (slice(None), slice(None), slice(128 * tile, 128 * tile + 128))
        z, sa = z_ref[at], sa_ref[at]
        x_out[at] = q0 * z + q1 * sa
        r_out[at] = q2 * r_ref[at] + q3 * na_ref[at] + q1 * nb_ref[at]
        p_out[at] = q2 * z + q3 * sa + q1 * sb_ref[at]


def per_device(observations, obs_noise, prior_noise, observed, kappa_sq, obs_precision):
    vmem = pl.BlockSpec(memory_space=pltpu.VMEM)
    hbm = pl.BlockSpec(memory_space=pl.ANY)
    out = jax.ShapeDtypeStruct(observations.shape, F32)

    def buf(*shape):
        return pltpu.VMEM(shape, F32)

    block = observations.shape
    parts = pl.pallas_call(
        kernel,
        out_shape=(out,) * 6 + (jax.ShapeDtypeStruct((8, 128), F32),),
        in_specs=[hbm] * 6,
        out_specs=(hbm,) * 6 + (vmem,),
        scratch_shapes=[
            buf(*block), buf(*block), buf(*block), pltpu.VMEM(block, jnp.int32),
            buf(*kappa_sq.shape), buf(*kappa_sq.shape),
            buf(*block), buf(*block), buf(*block), buf(*block), buf(*block), buf(*block),
            buf(128, 128), buf(128, 128), buf(128, 128), buf(128, 128),
            buf(128, 128), buf(LEVELS, 128, 128), buf(128, 128),
            buf(128, 128), buf(128, 128),
            buf(128, 128), buf(256, 128), buf(256, 128),
            buf(128, 128), buf(256, 128), buf(256, 128),
            buf(2, 256, 128), buf(2, 2, 8, 128), buf(2, 2, 8, 128), buf(2, 2, 16, 128),
            buf(64, 128), buf(64, 128), buf(8, 128), buf(8, 128),
            pltpu.SemaphoreType.DMA((5,)), pltpu.SemaphoreType.DMA((5,)),
            pltpu.SemaphoreType.DMA((8,)), pltpu.SemaphoreType.DMA((8,)),
            pltpu.SemaphoreType.DMA((2,)), pltpu.SemaphoreType.DMA((2,)),
            pltpu.SemaphoreType.DMA((5,)), pltpu.SemaphoreType.DMA((6,)),
            pltpu.SemaphoreType.DMA((6,)),
        ],
        compiler_params=pltpu.CompilerParams(collective_id=0, has_side_effects=True),
    )(observations, obs_noise, prior_noise, observed, kappa_sq, obs_precision)
    return pl.pallas_call(
        combine, out_shape=(out, out, out), in_specs=[vmem] * 7, out_specs=(vmem,) * 3
    )(*parts)


def solution(mesh):
    in_specs = (P("tm", "rows", None),) * 4 + (P("rows", None),) * 2
    out_specs = (P("tm", "rows", None),) * 3
    return jax.shard_map(
        per_device, mesh=mesh, in_specs=in_specs, out_specs=out_specs, check_vma=False
    )
```

```python
import jax
import jax.numpy as jnp
from jax import lax
from jax.experimental import pallas as pl
from jax.experimental.pallas import tpu as pltpu
from jax.sharding import PartitionSpec as P

RHO = 0.995
RHO_SQ = RHO * RHO
MESH = pl.DeviceIdType.MESH
F32 = jnp.float32
NT = 64
NY = 8


def patch_of(m):
    x, z, c = m // 16, (m // 2) % 8, m % 2
    odd = x % 2
    return 16 * x + 2 * (z + odd * (7 - 2 * z)) + c


def device_of(j):
    return patch_of(j)


def ring_tile(tile):
    return tile + (0, 0, 1, -1)[tile % 4]


def ring_order(v, tile):
    if tile % 4 < 2:
        return v
    axis = v.ndim - 2
    v = pltpu.roll(v, 4, axis)
    even = (iota(v.shape, axis) // 2) % 2 == 0
    return jnp.where(even, pltpu.roll(v, 6, axis), pltpu.roll(v, 2, axis))


def iota(shape, axis):
    return lax.broadcasted_iota(jnp.int32, shape, axis)


def swap_blocks(v):
    shape, sub, lane = v.shape, v.ndim - 2, v.ndim - 1
    s, g = iota(shape, sub), iota(shape, lane) // 16
    for b in (1, 2, 4):
        down = pltpu.roll(pltpu.roll(v, 8 - b, sub), 16 * b, lane)
        s_b, g_b = (s // b) % 2, (g // b) % 2
        if b == 4:
            v = jnp.where(s_b == g_b, v, down)
        else:
            up = pltpu.roll(pltpu.roll(v, b, sub), 128 - 16 * b, lane)
            v = jnp.where(s_b == g_b, v, jnp.where(s_b == 0, down, up))
    return v


def lane_sum(v):
    return jnp.sum(v, axis=1, keepdims=True)


def fold(v):
    return jnp.sum(v.reshape(v.shape[0] // 8, 8, 128), axis=0)


def kernel(
    obs_hbm, noise_hbm, prior_hbm, mask_hbm, kappa_hbm, prec_hbm,
    z_hbm, na_hbm, sa_hbm, nb_hbm, sb_hbm, r_hbm, coef_ref,
    obs_ref, noise_ref, prior_ref, mask_ref, kappa_ref, prec_ref,
    z_all, na_all, sa_all, nb_all, sb_all, r_all,
    s_mask, s_right, b_mask, b_right, down, joins, nc,
    s_z, s_one, s_two, b_z, b_one, b_two, pads, cols_out, side_in, rows_in,
    sums_y, sums_t, mine, one_row,
    send_big, recv_big, halo_send, halo_recv, sum_send, sum_recv, own_sem, in_sem, out_sem,
):
    me, y = lax.axis_index("tm"), lax.axis_index("rows")
    j = patch_of(me)

    barrier = pltpu.get_barrier_semaphore()

    def each_peer(act):
        def block(b, carry):
            base = me + 22 + 7 * b + jnp.where(b >= 6, 1, 0)
            base = base - jnp.where(base >= NT, NT, 0)
            base = base - jnp.where(base >= NT, NT, 0)
            for i in range(7):
                t = base + i
                act(t - jnp.where(t >= NT, NT, 0))
            return carry

        lax.fori_loop(0, 9, block, 0)

    def greet(t):
        pl.semaphore_signal(barrier, inc=1, device_id={"tm": t}, device_id_type=MESH)

    loads = [
        pltpu.make_async_copy(src, dst, in_sem.at[i])
        for i, (src, dst) in enumerate(
            (
                (mask_hbm, mask_ref),
                (obs_hbm, obs_ref),
                (noise_hbm, noise_ref),
                (prior_hbm, prior_ref),
                (prec_hbm, prec_ref),
                (kappa_hbm, kappa_ref),
            )
        )
    ]
    for load in loads:
        load.start()

    each_peer(greet)
    for k in range(1, NY):
        t = lax.rem(y + k, NY)
        pl.semaphore_signal(barrier, inc=1, device_id={"rows": t}, device_id_type=MESH)
    for load in loads:
        load.wait()

    for tile in range(8):
        cols = slice(128 * tile, 128 * tile + 128)
        mask = mask_ref[:, :, cols].astype(F32)
        prec = prec_ref[:, cols][None]
        right = mask * (prec * obs_ref[:, :, cols] + jnp.sqrt(prec) * noise_ref[:, :, cols])
        right = right + prior_ref[:, :, cols]
        r_all[:, :, cols] = right
        mask, right = ring_order(swap_blocks(mask), tile), ring_order(swap_blocks(right), tile)
        for h in range(2):
            at = pl.ds(16 * ring_tile(tile) + h, 8, stride=2)
            s_mask[at, :] = mask[h]
            s_right[at, :] = right[h]

    pl.semaphore_wait(barrier, NT - 1 + NY - 1)

    def to_all(src, dst, slot, rows):
        def send(t):
            pltpu.make_async_remote_copy(
                src_ref=src.at[pl.ds(rows * t, rows)],
                dst_ref=dst.at[pl.ds(rows * me, rows)],
                send_sem=send_big.at[slot],
                recv_sem=recv_big.at[slot],
                device_id={"tm": t},
                device_id_type=MESH,
            ).start()

        each_peer(send)
        own = pltpu.make_async_copy(
            src.at[pl.ds(rows * me, rows)], dst.at[pl.ds(rows * me, rows)], own_sem.at[slot]
        )
        own.start()
        return own

    def big(src, dst, slot, rows):
        n = rows * (NT - 1)
        return pltpu.make_async_remote_copy(
            src_ref=src.at[pl.ds(0, n)],
            dst_ref=dst.at[pl.ds(0, n)],
            send_sem=send_big.at[slot],
            recv_sem=recv_big.at[slot],
            device_id={"tm": lax.rem(me + 1, NT)},
            device_id_type=MESH,
        )

    own_mask = to_all(s_mask, b_mask, 0, 2)
    own_right = to_all(s_right, b_right, 1, 2)

    tile, back = j // 8, j % 8
    columns = pl.ds(pl.multiple_of(tile * 128, 128), 128)
    one_row[...] = swap_blocks(1.0 / (kappa_ref[:, columns] + 4.0))
    per_stencil = jnp.broadcast_to(one_row[pl.ds(back, 1), :], (8, 128))
    mine[...] = swap_blocks(prec_ref[:, columns])
    ratio = per_stencil * mine[pl.ds(back, 1), :]

    own_mask.wait()
    big(s_mask, b_mask, 0, 2).wait_recv()

    seg = iota((8, 128), 0)
    ones, zeros = jnp.ones((8, 128), F32), jnp.zeros((8, 128), F32)
    w = [b_mask[pl.ds(k, 8, stride=16), :] * ratio for k in range(16)]
    a, b, c, d = ones, zeros, zeros, ones
    for k in range(16):
        ac, bd = a + c, b + d
        a, b, c, d = w[k] * ac + RHO_SQ * a, w[k] * bd + RHO_SQ * b, ac, bd
    scale = 1.0 / (c + d)
    a, b, c, d = a * scale, b * scale, c * scale, d * scale
    for n in (1, 2, 4):
        pa, pb, pc, pd = [pltpu.roll(q, n, 0) for q in (a, b, c, d)]
        keep = seg < n
        a, b, c, d = [
            jnp.where(keep, old, new)
            for old, new in zip(
                (a, b, c, d),
                (a * pa + b * pc, a * pb + b * pd, c * pa + d * pc, c * pb + d * pd),
            )
        ]
    b = jnp.where(seg == 0, 0.0, pltpu.roll(b, 1, 0))
    d = jnp.where(seg == 0, 1.0, pltpu.roll(d, 1, 0))
    inverses = []
    for k in range(16):
        before_b, before_d = b, d
        bd = b + d
        b, d = w[k] * bd + RHO_SQ * b, bd
        inverse = d / (b + d)
        if k == 15:
            before = before_b / before_d
            final = w[k] + ((1.0 - RHO_SQ) + before) / (1.0 + before)
            inverse = jnp.where(seg == 7, 1.0 / final, inverse)
        inverses.append(inverse)
    carry = [RHO * inverse for inverse in inverses]
    carry[15] = jnp.where(seg == 7, 0.0, carry[15])
    into = pltpu.roll(carry[15], 1, 0)
    for k in range(16):
        down[0, k], down[1, k], down[2, k] = inverses[k], carry[k], into
        if k < 15:
            into = into * carry[k]
    back_in = carry[15]
    for k in range(15, -1, -1):
        down[3, k] = back_in
        if k > 0:
            back_in = back_in * carry[k - 1]
    for i, n in enumerate((1, 2, 4)):
        joins[i], joins[3 + i] = into, back_in
        into, back_in = into * pltpu.roll(into, n, 0), back_in * pltpu.roll(back_in, 8 - n, 0)

    def solve(load, keep):
        y, values = None, []
        for k in range(16):
            f = load(k) * per_stencil
            y = f if k == 0 else f + down[1, k - 1] * y
            values.append(y)
        for i, n in enumerate((1, 2, 4)):
            y = y + joins[i] * pltpu.roll(y, n, 0)
        y = pltpu.roll(y, 1, 0)
        values = [(v + down[2, k] * y) * down[0, k] for k, v in enumerate(values)]
        for k in range(14, -1, -1):
            values[k] = values[k] + down[1, k] * values[k + 1]
        z = values[0]
        for i, n in enumerate((1, 2, 4)):
            z = z + joins[3 + i] * pltpu.roll(z, 8 - n, 0)
        z = pltpu.roll(z, 7, 0)
        for k in range(16):
            values[k] = values[k] + down[3, k] * z
            keep(k, values[k])
        return values

    left, right_dev = device_of(lax.rem(j + NT - 1, NT)), device_of(lax.rem(j + 1, NT))
    above, below = lax.rem(y + NY - 1, NY), lax.rem(y + 1, NY)

    def halo_copies(n):
        pad = pads.at[n]
        parts = (
            (pad.at[pl.ds(8, 16)], rows_in.at[n, 1], {"rows": above}),
            (pad.at[pl.ds(32 * 7 + 8, 16)], rows_in.at[n, 0], {"rows": below}),
            (cols_out.at[n, 0], side_in.at[n, 1], {"tm": left}),
            (cols_out.at[n, 1], side_in.at[n, 0], {"tm": right_dev}),
        )
        return [
            pltpu.make_async_remote_copy(
                src_ref=src,
                dst_ref=dst,
                send_sem=halo_send.at[4 * n + i],
                recv_sem=halo_recv.at[4 * n + i],
                device_id=to,
                device_id_type=MESH,
            )
            for i, (src, dst, to) in enumerate(parts)
        ]

    def halo_start(n, v):
        for r in range(8):
            pads[n, pl.ds(32 * r + 8, 16), :] = v[16 * r : 16 * r + 16]
        cols_out[n, 0] = pads[n, pl.ds(8, 8, stride=32), :]
        cols_out[n, 1] = pads[n, pl.ds(23, 8, stride=32), :]
        copies = halo_copies(n)
        for copy in copies:
            copy.start()
        return copies

    hour = iota((16, 128), 1)
    from_before = jnp.where(hour == 0, 0.0, RHO).astype(F32)
    from_after = jnp.where(hour == 127, 0.0, RHO).astype(F32)
    weight = jnp.where((hour == 0) | (hour == 127), 1.0, 1.0 + RHO_SQ).astype(F32)

    def neighbours(n, copies):
        for copy in copies:
            copy.wait_recv()
        pads[n, pl.ds(7, 8, stride=32), :] = jnp.where(j == 0, 0.0, side_in[n, 0])
        pads[n, pl.ds(24, 8, stride=32), :] = jnp.where(j == NT - 1, 0.0, side_in[n, 1])
        for r in range(8):
            if r == 0:
                up = jnp.where(y == 0, 0.0, rows_in[n, 0])
            else:
                up = pads[n, pl.ds(32 * (r - 1) + 8, 16), :]
            if r == 7:
                down = jnp.where(y == NY - 1, 0.0, rows_in[n, 1])
            else:
                down = pads[n, pl.ds(32 * (r + 1) + 8, 16), :]
            u = pads[n, pl.ds(32 * r + 7, 16), :] + pads[n, pl.ds(32 * r + 9, 16), :]
            u = u + (up + down)
            u = weight * u - (
                from_before * pltpu.roll(u, 1, 1) + from_after * pltpu.roll(u, 127, 1)
            )
            nc[pl.ds(16 * r, 16), :] = u
        return nc[...]

    own_right.wait()
    big(s_right, b_right, 1, 2).wait_recv()
    def right_at(k):
        return b_right[pl.ds(k, 8, stride=16), :]

    def keep_z(k, v):
        s_z[pl.ds(k, 8, stride=16), :] = v

    def total_of(load, values):
        return sum(load(k) * v for k, v in enumerate(values))

    z_values = solve(right_at, keep_z)
    copies_0 = halo_start(0, s_z[...].T)
    rz_part = total_of(right_at, z_values)

    def pair(ref, n):
        ref[pl.ds(0, 128, stride=2), :] = n.T

        def load(k):
            return ref[pl.ds(2 * k, 8, stride=32), :]

        def keep(k, v):
            ref[pl.ds(2 * k + 1, 8, stride=32), :] = v

        return load, solve(load, keep)

    n0 = neighbours(0, copies_0)
    load_0, s_values = pair(s_one, n0)
    copies_1 = halo_start(1, s_one[pl.ds(1, 128, stride=2), :].T)
    own_z = to_all(s_z, b_z, 2, 2)
    own_one = to_all(s_one, b_one, 3, 4)
    e1_part = total_of(right_at, s_values)
    e2_part = total_of(load_0, s_values)

    n1 = neighbours(1, copies_1)
    e3_part = fold(n1 * jnp.concatenate([pads[1, pl.ds(32 * r + 8, 16), :] for r in range(8)], axis=0))

    sub = iota((8, 128), 0)
    total = jnp.zeros((8, 128), F32)
    for i, part in enumerate((rz_part, e1_part, e2_part, e3_part)):
        total = jnp.where(sub == i, jnp.sum(part, axis=0, keepdims=True), total)
    total = total + pltpu.roll(total, 64, 1)
    total = total + pltpu.roll(total, 32, 1)
    total = jnp.where(iota((8, 128), 1) // 32 == sub, total, 0.0)
    one_row[...] = jnp.broadcast_to(jnp.sum(total, axis=0, keepdims=True), (8, 128))
    sums_t[pl.ds(me, 1), :] = one_row[0:1, :]

    def send_sum(t):
        pltpu.make_async_remote_copy(
            src_ref=one_row.at[pl.ds(0, 1)],
            dst_ref=sums_t.at[pl.ds(me, 1)],
            send_sem=sum_send.at[1],
            recv_sem=sum_recv.at[1],
            device_id={"tm": t},
            device_id_type=MESH,
        ).start()

    each_peer(send_sum)

    pair(s_two, n1)
    own_two = to_all(s_two, b_two, 4, 4)

    def all_rows(n, src, dst, slot):
        return pltpu.make_async_remote_copy(
            src_ref=src.at[pl.ds(0, n)],
            dst_ref=dst.at[pl.ds(0, n)],
            send_sem=sum_send.at[slot],
            recv_sem=sum_recv.at[slot],
            device_id={"rows": lax.rem(y + 1, NY)},
            device_id_type=MESH,
        )

    all_rows(NT - 1, sums_t, sums_t, 1).wait_recv()
    mine[...] = fold(sums_t[...])
    sums_y[pl.ds(pl.multiple_of(8 * y, 8), 8), :] = mine[...]
    for k in range(1, NY):
        pltpu.make_async_remote_copy(
            src_ref=mine,
            dst_ref=sums_y.at[pl.ds(pl.multiple_of(8 * y, 8), 8)],
            send_sem=sum_send.at[0],
            recv_sem=sum_recv.at[0],
            device_id={"rows": lax.rem(y + k, NY)},
            device_id_type=MESH,
        ).start()

    stores = []
    store = pltpu.make_async_copy(r_all, r_hbm, out_sem.at[5])
    store.start()
    stores.append(store)
    outs = (
        (0, b_z, 2, 0, z_all, z_hbm),
        (1, b_one, 4, 0, na_all, na_hbm),
        (2, b_one, 4, 1, sa_all, sa_hbm),
        (3, b_two, 4, 0, nb_all, nb_hbm),
        (4, b_two, 4, 1, sb_all, sb_hbm),
    )
    for i, ref, stride, o, dst, hbm in outs:
        if i == 0:
            own_z.wait()
            big(s_z, b_z, 2, 2).wait_recv()
        elif i == 1:
            own_one.wait()
            big(s_one, b_one, 3, 4).wait_recv()
        elif i == 3:
            own_two.wait()
            big(s_two, b_two, 4, 4).wait_recv()
        for tile in range(8):
            for h in range(2):
                at = pl.ds(8 * stride * ring_tile(tile) + h * (stride // 2) + o, 8, stride=stride)
                dst[h, :, 128 * tile : 128 * tile + 128] = swap_blocks(ring_order(ref[at, :], tile))
        store = pltpu.make_async_copy(dst, hbm, out_sem.at[i])
        store.start()
        stores.append(store)

    all_rows(8 * (NY - 1), sums_y, sums_y, 0).wait_recv()
    sums = jnp.sum(fold(sums_y[...]), axis=0, keepdims=True)
    group = iota((1, 128), 1) // 32
    rz0, e1, e2, e3 = [lane_sum(jnp.where(group == i, sums, 0.0)) for i in range(4)]
    curved = rz0 - e1
    alpha0 = rz0 / curved
    beta0 = (e2 * rz0 - e1 * e1) / (curved * curved)
    along = 1.0 + beta0 - alpha0
    curved1 = along * along * curved + 2.0 * along * alpha0 * (e1 - e2) + alpha0 * alpha0 * (e2 - e3)
    alpha1 = beta0 * rz0 / curved1
    first = alpha0 + alpha1 * (1.0 + beta0)
    second = alpha0 * alpha1
    c0, c1 = 1.0 - first + second, first - 2.0 * second

    row = iota((8, 128), 0)
    coef_ref[...] = jnp.where(
        row == 0,
        first - second,
        jnp.where(row == 1, second, jnp.where(row == 2, c0, c1)),
    )
    for store in stores:
        store.wait()
    for copy in copies_0 + copies_1:
        copy.wait_send()
    big(s_mask, b_mask, 0, 2).wait_send()
    big(s_right, b_right, 1, 2).wait_send()
    big(s_z, b_z, 2, 2).wait_send()
    big(s_one, b_one, 3, 4).wait_send()
    big(s_two, b_two, 4, 4).wait_send()
    all_rows(8 * (NY - 1), sums_y, sums_y, 0).wait_send()
    all_rows(NT - 1, sums_t, sums_t, 1).wait_send()


def combine(z_ref, na_ref, sa_ref, nb_ref, sb_ref, r_ref, coef_ref, x_out, r_out, p_out):
    q0, q1, q2, q3 = [coef_ref[i : i + 1, 0:1].reshape(1, 1, 1) for i in range(4)]
    for tile in range(8):
        at = (slice(None), slice(None), slice(128 * tile, 128 * tile + 128))
        z, sa = z_ref[at], sa_ref[at]
        x_out[at] = q0 * z + q1 * sa
        r_out[at] = q2 * r_ref[at] + q3 * na_ref[at] + q1 * nb_ref[at]
        p_out[at] = q2 * z + q3 * sa + q1 * sb_ref[at]


def per_device(observations, obs_noise, prior_noise, observed, kappa_sq, obs_precision):
    vmem = pl.BlockSpec(memory_space=pltpu.VMEM)
    hbm = pl.BlockSpec(memory_space=pl.ANY)
    out = jax.ShapeDtypeStruct(observations.shape, F32)

    def buf(*shape):
        return pltpu.VMEM(shape, F32)

    block = observations.shape
    parts = pl.pallas_call(
        kernel,
        out_shape=(out,) * 6 + (jax.ShapeDtypeStruct((8, 128), F32),),
        in_specs=[hbm] * 6,
        out_specs=(hbm,) * 6 + (vmem,),
        scratch_shapes=[
            buf(*block), buf(*block), buf(*block), pltpu.VMEM(block, jnp.int32),
            buf(*kappa_sq.shape), buf(*kappa_sq.shape),
            buf(*block), buf(*block), buf(*block), buf(*block), buf(*block), buf(*block),
            buf(128, 128), buf(128, 128), buf(128, 128), buf(128, 128),
            buf(4, 16, 8, 128), buf(6, 8, 128), buf(128, 128),
            buf(128, 128), buf(256, 128), buf(256, 128),
            buf(128, 128), buf(256, 128), buf(256, 128),
            buf(2, 256, 128), buf(2, 2, 8, 128), buf(2, 2, 8, 128), buf(2, 2, 16, 128),
            buf(64, 128), buf(64, 128), buf(8, 128), buf(8, 128),
            pltpu.SemaphoreType.DMA((5,)), pltpu.SemaphoreType.DMA((5,)),
            pltpu.SemaphoreType.DMA((8,)), pltpu.SemaphoreType.DMA((8,)),
            pltpu.SemaphoreType.DMA((2,)), pltpu.SemaphoreType.DMA((2,)),
            pltpu.SemaphoreType.DMA((5,)), pltpu.SemaphoreType.DMA((6,)),
            pltpu.SemaphoreType.DMA((6,)),
        ],
        compiler_params=pltpu.CompilerParams(collective_id=0, has_side_effects=True),
    )(observations, obs_noise, prior_noise, observed, kappa_sq, obs_precision)
    return pl.pallas_call(
        combine, out_shape=(out, out, out), in_specs=[vmem] * 7, out_specs=(vmem,) * 3
    )(*parts)


def solution(mesh):
    in_specs = (P("tm", "rows", None),) * 4 + (P("rows", None),) * 2
    out_specs = (P("tm", "rows", None),) * 3
    return jax.shard_map(
        per_device, mesh=mesh, in_specs=in_specs, out_specs=out_specs, check_vma=False
    )
```

```python
import jax
import jax.numpy as jnp
from jax import lax
from jax.experimental import pallas as pl
from jax.experimental.pallas import tpu as pltpu
from jax.sharding import PartitionSpec as P

RHO = 0.995
RHO_SQ = RHO * RHO
MESH = pl.DeviceIdType.MESH
F32 = jnp.float32
NT = 64
NY = 8


def patch_of(m):
    x, z, c = m // 16, (m // 2) % 8, m % 2
    odd = x % 2
    return 16 * x + 2 * (z + odd * (7 - 2 * z)) + c


def device_of(j):
    return patch_of(j)


def ring_tile(tile):
    return tile + (0, 0, 1, -1)[tile % 4]


def ring_order(v, tile):
    if tile % 4 < 2:
        return v
    axis = v.ndim - 2
    v = pltpu.roll(v, 4, axis)
    even = (iota(v.shape, axis) // 2) % 2 == 0
    return jnp.where(even, pltpu.roll(v, 6, axis), pltpu.roll(v, 2, axis))


def iota(shape, axis):
    return lax.broadcasted_iota(jnp.int32, shape, axis)


def swap_blocks(v):
    shape, sub, lane = v.shape, v.ndim - 2, v.ndim - 1
    s, g = iota(shape, sub), iota(shape, lane) // 16
    for b in (1, 2, 4):
        down = pltpu.roll(pltpu.roll(v, 8 - b, sub), 16 * b, lane)
        s_b, g_b = (s // b) % 2, (g // b) % 2
        if b == 4:
            v = jnp.where(s_b == g_b, v, down)
        else:
            up = pltpu.roll(pltpu.roll(v, b, sub), 128 - 16 * b, lane)
            v = jnp.where(s_b == g_b, v, jnp.where(s_b == 0, down, up))
    return v


def lane_sum(v):
    return jnp.sum(v, axis=1, keepdims=True)


def fold(v):
    return jnp.sum(v.reshape(v.shape[0] // 8, 8, 128), axis=0)


def kernel(
    obs_hbm, noise_hbm, prior_hbm, mask_hbm, kappa_hbm, prec_hbm,
    z_all, na_all, sa_all, nb_all, sb_all, r_all, coef_ref,
    obs_ref, noise_ref, prior_ref, mask_ref, kappa_ref, prec_ref,
    s_mask, s_right, b_mask, b_right, down, joins, nc,
    s_z, s_one, s_two, b_z, b_one, b_two, pads, cols_out, side_in, rows_in,
    sums_y, sums_t, mine, one_row,
    send_big, recv_big, halo_send, halo_recv, sum_send, sum_recv, own_sem, in_sem,
):
    me, y = lax.axis_index("tm"), lax.axis_index("rows")
    j = patch_of(me)

    barrier = pltpu.get_barrier_semaphore()

    def each_peer(act):
        def block(b, carry):
            base = me + 22 + 7 * b + jnp.where(b >= 6, 1, 0)
            base = base - jnp.where(base >= NT, NT, 0)
            base = base - jnp.where(base >= NT, NT, 0)
            for i in range(7):
                t = base + i
                act(t - jnp.where(t >= NT, NT, 0))
            return carry

        lax.fori_loop(0, 9, block, 0)

    def greet(t):
        pl.semaphore_signal(barrier, inc=1, device_id={"tm": t}, device_id_type=MESH)

    loads = [
        pltpu.make_async_copy(src, dst, in_sem.at[i])
        for i, (src, dst) in enumerate(
            (
                (mask_hbm, mask_ref),
                (obs_hbm, obs_ref),
                (noise_hbm, noise_ref),
                (prior_hbm, prior_ref),
                (prec_hbm, prec_ref),
                (kappa_hbm, kappa_ref),
            )
        )
    ]
    for load in loads:
        load.start()

    each_peer(greet)
    for k in range(1, NY):
        t = lax.rem(y + k, NY)
        pl.semaphore_signal(barrier, inc=1, device_id={"rows": t}, device_id_type=MESH)
    for load in loads:
        load.wait()

    for tile in range(8):
        cols = slice(128 * tile, 128 * tile + 128)
        mask = mask_ref[:, :, cols].astype(F32)
        prec = prec_ref[:, cols][None]
        right = mask * (prec * obs_ref[:, :, cols] + jnp.sqrt(prec) * noise_ref[:, :, cols])
        right = right + prior_ref[:, :, cols]
        r_all[:, :, cols] = right
        mask, right = ring_order(swap_blocks(mask), tile), ring_order(swap_blocks(right), tile)
        for h in range(2):
            at = pl.ds(16 * ring_tile(tile) + h, 8, stride=2)
            s_mask[at, :] = mask[h]
            s_right[at, :] = right[h]

    pl.semaphore_wait(barrier, NT - 1 + NY - 1)

    def to_all(src, dst, slot, rows):
        def send(t):
            pltpu.make_async_remote_copy(
                src_ref=src.at[pl.ds(rows * t, rows)],
                dst_ref=dst.at[pl.ds(rows * me, rows)],
                send_sem=send_big.at[slot],
                recv_sem=recv_big.at[slot],
                device_id={"tm": t},
                device_id_type=MESH,
            ).start()

        each_peer(send)
        own = pltpu.make_async_copy(
            src.at[pl.ds(rows * me, rows)], dst.at[pl.ds(rows * me, rows)], own_sem.at[slot]
        )
        own.start()
        return own

    def big(src, dst, slot, rows):
        n = rows * (NT - 1)
        return pltpu.make_async_remote_copy(
            src_ref=src.at[pl.ds(0, n)],
            dst_ref=dst.at[pl.ds(0, n)],
            send_sem=send_big.at[slot],
            recv_sem=recv_big.at[slot],
            device_id={"tm": lax.rem(me + 1, NT)},
            device_id_type=MESH,
        )

    own_mask = to_all(s_mask, b_mask, 0, 2)
    own_right = to_all(s_right, b_right, 1, 2)

    tile, back = j // 8, j % 8
    columns = pl.ds(pl.multiple_of(tile * 128, 128), 128)
    one_row[...] = swap_blocks(1.0 / (kappa_ref[:, columns] + 4.0))
    per_stencil = jnp.broadcast_to(one_row[pl.ds(back, 1), :], (8, 128))
    mine[...] = swap_blocks(prec_ref[:, columns])
    ratio = per_stencil * mine[pl.ds(back, 1), :]

    own_mask.wait()
    big(s_mask, b_mask, 0, 2).wait_recv()

    seg = iota((8, 128), 0)
    ones, zeros = jnp.ones((8, 128), F32), jnp.zeros((8, 128), F32)
    w = [b_mask[pl.ds(k, 8, stride=16), :] * ratio for k in range(16)]
    a, b, c, d = ones, zeros, zeros, ones
    for k in range(16):
        ac, bd = a + c, b + d
        a, b, c, d = w[k] * ac + RHO_SQ * a, w[k] * bd + RHO_SQ * b, ac, bd
    scale = 1.0 / (c + d)
    a, b, c, d = a * scale, b * scale, c * scale, d * scale
    for n in (1, 2, 4):
        pa, pb, pc, pd = [pltpu.roll(q, n, 0) for q in (a, b, c, d)]
        keep = seg < n
        a, b, c, d = [
            jnp.where(keep, old, new)
            for old, new in zip(
                (a, b, c, d),
                (a * pa + b * pc, a * pb + b * pd, c * pa + d * pc, c * pb + d * pd),
            )
        ]
    b = jnp.where(seg == 0, 0.0, pltpu.roll(b, 1, 0))
    d = jnp.where(seg == 0, 1.0, pltpu.roll(d, 1, 0))
    inverses = []
    for k in range(16):
        before_b, before_d = b, d
        bd = b + d
        b, d = w[k] * bd + RHO_SQ * b, bd
        inverse = d / (b + d)
        if k == 15:
            before = before_b / before_d
            final = w[k] + ((1.0 - RHO_SQ) + before) / (1.0 + before)
            inverse = jnp.where(seg == 7, 1.0 / final, inverse)
        inverses.append(inverse)
    carry = [RHO * inverse for inverse in inverses]
    carry[15] = jnp.where(seg == 7, 0.0, carry[15])
    into = pltpu.roll(carry[15], 1, 0)
    for k in range(16):
        down[0, k], down[1, k], down[2, k] = inverses[k], carry[k], into
        if k < 15:
            into = into * carry[k]
    back_in = carry[15]
    for k in range(15, -1, -1):
        down[3, k] = back_in
        if k > 0:
            back_in = back_in * carry[k - 1]
    for i, n in enumerate((1, 2, 4)):
        joins[i], joins[3 + i] = into, back_in
        into, back_in = into * pltpu.roll(into, n, 0), back_in * pltpu.roll(back_in, 8 - n, 0)

    def solve(load, keep):
        y, values = None, []
        for k in range(16):
            f = load(k) * per_stencil
            y = f if k == 0 else f + down[1, k - 1] * y
            values.append(y)
        for i, n in enumerate((1, 2, 4)):
            y = y + joins[i] * pltpu.roll(y, n, 0)
        y = pltpu.roll(y, 1, 0)
        values = [(v + down[2, k] * y) * down[0, k] for k, v in enumerate(values)]
        for k in range(14, -1, -1):
            values[k] = values[k] + down[1, k] * values[k + 1]
        z = values[0]
        for i, n in enumerate((1, 2, 4)):
            z = z + joins[3 + i] * pltpu.roll(z, 8 - n, 0)
        z = pltpu.roll(z, 7, 0)
        for k in range(16):
            values[k] = values[k] + down[3, k] * z
            keep(k, values[k])
        return values

    left, right_dev = device_of(lax.rem(j + NT - 1, NT)), device_of(lax.rem(j + 1, NT))
    above, below = lax.rem(y + NY - 1, NY), lax.rem(y + 1, NY)

    def halo_copies(n):
        pad = pads.at[n]
        parts = (
            (pad.at[pl.ds(8, 16)], rows_in.at[n, 1], {"rows": above}),
            (pad.at[pl.ds(32 * 7 + 8, 16)], rows_in.at[n, 0], {"rows": below}),
            (cols_out.at[n, 0], side_in.at[n, 1], {"tm": left}),
            (cols_out.at[n, 1], side_in.at[n, 0], {"tm": right_dev}),
        )
        return [
            pltpu.make_async_remote_copy(
                src_ref=src,
                dst_ref=dst,
                send_sem=halo_send.at[4 * n + i],
                recv_sem=halo_recv.at[4 * n + i],
                device_id=to,
                device_id_type=MESH,
            )
            for i, (src, dst, to) in enumerate(parts)
        ]

    def halo_start(n, v):
        for r in range(8):
            pads[n, pl.ds(32 * r + 8, 16), :] = v[16 * r : 16 * r + 16]
        cols_out[n, 0] = pads[n, pl.ds(8, 8, stride=32), :]
        cols_out[n, 1] = pads[n, pl.ds(23, 8, stride=32), :]
        copies = halo_copies(n)
        for copy in copies:
            copy.start()
        return copies

    hour = iota((16, 128), 1)
    from_before = jnp.where(hour == 0, 0.0, RHO).astype(F32)
    from_after = jnp.where(hour == 127, 0.0, RHO).astype(F32)
    weight = jnp.where((hour == 0) | (hour == 127), 1.0, 1.0 + RHO_SQ).astype(F32)

    def neighbours(n, copies):
        for copy in copies:
            copy.wait_recv()
        pads[n, pl.ds(7, 8, stride=32), :] = jnp.where(j == 0, 0.0, side_in[n, 0])
        pads[n, pl.ds(24, 8, stride=32), :] = jnp.where(j == NT - 1, 0.0, side_in[n, 1])
        for r in range(8):
            if r == 0:
                up = jnp.where(y == 0, 0.0, rows_in[n, 0])
            else:
                up = pads[n, pl.ds(32 * (r - 1) + 8, 16), :]
            if r == 7:
                down = jnp.where(y == NY - 1, 0.0, rows_in[n, 1])
            else:
                down = pads[n, pl.ds(32 * (r + 1) + 8, 16), :]
            u = pads[n, pl.ds(32 * r + 7, 16), :] + pads[n, pl.ds(32 * r + 9, 16), :]
            u = u + (up + down)
            u = weight * u - (
                from_before * pltpu.roll(u, 1, 1) + from_after * pltpu.roll(u, 127, 1)
            )
            nc[pl.ds(16 * r, 16), :] = u
        return nc[...]

    own_right.wait()
    big(s_right, b_right, 1, 2).wait_recv()
    def right_at(k):
        return b_right[pl.ds(k, 8, stride=16), :]

    def keep_z(k, v):
        s_z[pl.ds(k, 8, stride=16), :] = v

    def total_of(load, values):
        return sum(load(k) * v for k, v in enumerate(values))

    z_values = solve(right_at, keep_z)
    copies_0 = halo_start(0, s_z[...].T)
    rz_part = total_of(right_at, z_values)

    def pair(ref, n):
        ref[pl.ds(0, 128, stride=2), :] = n.T

        def load(k):
            return ref[pl.ds(2 * k, 8, stride=32), :]

        def keep(k, v):
            ref[pl.ds(2 * k + 1, 8, stride=32), :] = v

        return load, solve(load, keep)

    n0 = neighbours(0, copies_0)
    load_0, s_values = pair(s_one, n0)
    copies_1 = halo_start(1, s_one[pl.ds(1, 128, stride=2), :].T)
    own_z = to_all(s_z, b_z, 2, 2)
    own_one = to_all(s_one, b_one, 3, 4)
    e1_part = total_of(right_at, s_values)
    e2_part = total_of(load_0, s_values)

    n1 = neighbours(1, copies_1)
    e3_part = fold(n1 * jnp.concatenate([pads[1, pl.ds(32 * r + 8, 16), :] for r in range(8)], axis=0))

    sub = iota((8, 128), 0)
    total = jnp.zeros((8, 128), F32)
    for i, part in enumerate((rz_part, e1_part, e2_part, e3_part)):
        total = jnp.where(sub == i, jnp.sum(part, axis=0, keepdims=True), total)
    total = total + pltpu.roll(total, 64, 1)
    total = total + pltpu.roll(total, 32, 1)
    total = jnp.where(iota((8, 128), 1) // 32 == sub, total, 0.0)
    one_row[...] = jnp.broadcast_to(jnp.sum(total, axis=0, keepdims=True), (8, 128))
    sums_t[pl.ds(me, 1), :] = one_row[0:1, :]

    def send_sum(t):
        pltpu.make_async_remote_copy(
            src_ref=one_row.at[pl.ds(0, 1)],
            dst_ref=sums_t.at[pl.ds(me, 1)],
            send_sem=sum_send.at[1],
            recv_sem=sum_recv.at[1],
            device_id={"tm": t},
            device_id_type=MESH,
        ).start()

    each_peer(send_sum)

    pair(s_two, n1)
    own_two = to_all(s_two, b_two, 4, 4)

    def all_rows(n, src, dst, slot):
        return pltpu.make_async_remote_copy(
            src_ref=src.at[pl.ds(0, n)],
            dst_ref=dst.at[pl.ds(0, n)],
            send_sem=sum_send.at[slot],
            recv_sem=sum_recv.at[slot],
            device_id={"rows": lax.rem(y + 1, NY)},
            device_id_type=MESH,
        )

    all_rows(NT - 1, sums_t, sums_t, 1).wait_recv()
    mine[...] = fold(sums_t[...])
    sums_y[pl.ds(pl.multiple_of(8 * y, 8), 8), :] = mine[...]
    for k in range(1, NY):
        pltpu.make_async_remote_copy(
            src_ref=mine,
            dst_ref=sums_y.at[pl.ds(pl.multiple_of(8 * y, 8), 8)],
            send_sem=sum_send.at[0],
            recv_sem=sum_recv.at[0],
            device_id={"rows": lax.rem(y + k, NY)},
            device_id_type=MESH,
        ).start()

    outs = (
        (0, b_z, 2, 0, z_all),
        (1, b_one, 4, 0, na_all),
        (2, b_one, 4, 1, sa_all),
        (3, b_two, 4, 0, nb_all),
        (4, b_two, 4, 1, sb_all),
    )
    for i, ref, stride, o, dst in outs:
        if i == 0:
            own_z.wait()
            big(s_z, b_z, 2, 2).wait_recv()
        elif i == 1:
            own_one.wait()
            big(s_one, b_one, 3, 4).wait_recv()
        elif i == 3:
            own_two.wait()
            big(s_two, b_two, 4, 4).wait_recv()
        for tile in range(8):
            for h in range(2):
                at = pl.ds(8 * stride * ring_tile(tile) + h * (stride // 2) + o, 8, stride=stride)
                dst[h, :, 128 * tile : 128 * tile + 128] = swap_blocks(ring_order(ref[at, :], tile))

    all_rows(8 * (NY - 1), sums_y, sums_y, 0).wait_recv()
    sums = jnp.sum(fold(sums_y[...]), axis=0, keepdims=True)
    group = iota((1, 128), 1) // 32
    rz0, e1, e2, e3 = [lane_sum(jnp.where(group == i, sums, 0.0)) for i in range(4)]
    curved = rz0 - e1
    alpha0 = rz0 / curved
    beta0 = (e2 * rz0 - e1 * e1) / (curved * curved)
    along = 1.0 + beta0 - alpha0
    curved1 = along * along * curved + 2.0 * along * alpha0 * (e1 - e2) + alpha0 * alpha0 * (e2 - e3)
    alpha1 = beta0 * rz0 / curved1
    first = alpha0 + alpha1 * (1.0 + beta0)
    second = alpha0 * alpha1
    c0, c1 = 1.0 - first + second, first - 2.0 * second

    row = iota((8, 128), 0)
    coef_ref[...] = jnp.where(
        row == 0,
        first - second,
        jnp.where(row == 1, second, jnp.where(row == 2, c0, c1)),
    )
    for copy in copies_0 + copies_1:
        copy.wait_send()
    big(s_mask, b_mask, 0, 2).wait_send()
    big(s_right, b_right, 1, 2).wait_send()
    big(s_z, b_z, 2, 2).wait_send()
    big(s_one, b_one, 3, 4).wait_send()
    big(s_two, b_two, 4, 4).wait_send()
    all_rows(8 * (NY - 1), sums_y, sums_y, 0).wait_send()
    all_rows(NT - 1, sums_t, sums_t, 1).wait_send()


def combine(z_ref, na_ref, sa_ref, nb_ref, sb_ref, r_ref, coef_ref, x_out, r_out, p_out):
    q0, q1, q2, q3 = [coef_ref[i : i + 1, 0:1].reshape(1, 1, 1) for i in range(4)]
    for tile in range(8):
        at = (slice(None), slice(None), slice(128 * tile, 128 * tile + 128))
        z, sa = z_ref[at], sa_ref[at]
        x_out[at] = q0 * z + q1 * sa
        r_out[at] = q2 * r_ref[at] + q3 * na_ref[at] + q1 * nb_ref[at]
        p_out[at] = q2 * z + q3 * sa + q1 * sb_ref[at]


def per_device(observations, obs_noise, prior_noise, observed, kappa_sq, obs_precision):
    vmem = pl.BlockSpec(memory_space=pltpu.VMEM)
    hbm = pl.BlockSpec(memory_space=pl.ANY)
    out = jax.ShapeDtypeStruct(observations.shape, F32)

    def buf(*shape):
        return pltpu.VMEM(shape, F32)

    block = observations.shape
    parts = pl.pallas_call(
        kernel,
        out_shape=(buf(*block),) * 6 + (buf(8, 128),),
        in_specs=[hbm] * 6,
        out_specs=(vmem,) * 7,
        scratch_shapes=[
            buf(*block), buf(*block), buf(*block), pltpu.VMEM(block, jnp.int32),
            buf(*kappa_sq.shape), buf(*kappa_sq.shape),
            buf(128, 128), buf(128, 128), buf(128, 128), buf(128, 128),
            buf(4, 16, 8, 128), buf(6, 8, 128), buf(128, 128),
            buf(128, 128), buf(256, 128), buf(256, 128),
            buf(128, 128), buf(256, 128), buf(256, 128),
            buf(2, 256, 128), buf(2, 2, 8, 128), buf(2, 2, 8, 128), buf(2, 2, 16, 128),
            buf(64, 128), buf(64, 128), buf(8, 128), buf(8, 128),
            pltpu.SemaphoreType.DMA((5,)), pltpu.SemaphoreType.DMA((5,)),
            pltpu.SemaphoreType.DMA((8,)), pltpu.SemaphoreType.DMA((8,)),
            pltpu.SemaphoreType.DMA((2,)), pltpu.SemaphoreType.DMA((2,)),
            pltpu.SemaphoreType.DMA((5,)), pltpu.SemaphoreType.DMA((6,)),
        ],
        compiler_params=pltpu.CompilerParams(collective_id=0, has_side_effects=True),
    )(observations, obs_noise, prior_noise, observed, kappa_sq, obs_precision)
    return pl.pallas_call(
        combine, out_shape=(out, out, out), in_specs=[vmem] * 7, out_specs=(vmem,) * 3
    )(*[pltpu.with_memory_space_constraint(part, pltpu.VMEM) for part in parts])


def solution(mesh):
    in_specs = (P("tm", "rows", None),) * 4 + (P("rows", None),) * 2
    out_specs = (P("tm", "rows", None),) * 3
    return jax.shard_map(
        per_device, mesh=mesh, in_specs=in_specs, out_specs=out_specs, check_vma=False
    )
```

```python
import jax
import jax.numpy as jnp
from jax import lax
from jax.experimental import pallas as pl
from jax.experimental.pallas import tpu as pltpu
from jax.sharding import PartitionSpec as P

RHO = 0.995
RHO_SQ = RHO * RHO
MESH = pl.DeviceIdType.MESH
F32 = jnp.float32
NT = 64
NY = 8


def hops(o):
    z, x = (o // 2) % 8, o // 16
    return min(z, 8 - z) + min(x, 4 - x)


FAR_FIRST = sorted(range(1, NT), key=lambda o: (-hops(o), o))


def patch_of(m):
    x, z, c = m // 16, (m // 2) % 8, m % 2
    odd = x % 2
    return 16 * x + 2 * (z + odd * (7 - 2 * z)) + c


def device_of(j):
    return patch_of(j)


def ring_tile(tile):
    return tile + (0, 0, 1, -1)[tile % 4]


def ring_order(v, tile):
    if tile % 4 < 2:
        return v
    axis = v.ndim - 2
    v = pltpu.roll(v, 4, axis)
    even = (iota(v.shape, axis) // 2) % 2 == 0
    return jnp.where(even, pltpu.roll(v, 6, axis), pltpu.roll(v, 2, axis))


def iota(shape, axis):
    return lax.broadcasted_iota(jnp.int32, shape, axis)


def swap_blocks(v):
    shape, sub, lane = v.shape, v.ndim - 2, v.ndim - 1
    s, g = iota(shape, sub), iota(shape, lane) // 16
    for b in (1, 2, 4):
        down = pltpu.roll(pltpu.roll(v, 8 - b, sub), 16 * b, lane)
        s_b, g_b = (s // b) % 2, (g // b) % 2
        if b == 4:
            v = jnp.where(s_b == g_b, v, down)
        else:
            up = pltpu.roll(pltpu.roll(v, b, sub), 128 - 16 * b, lane)
            v = jnp.where(s_b == g_b, v, jnp.where(s_b == 0, down, up))
    return v


def lane_sum(v):
    return jnp.sum(v, axis=1, keepdims=True)


def fold(v):
    return jnp.sum(v.reshape(v.shape[0] // 8, 8, 128), axis=0)


def kernel(
    obs_hbm, noise_hbm, prior_hbm, mask_hbm, kappa_hbm, prec_hbm,
    z_all, na_all, sa_all, nb_all, sb_all, r_all, coef_ref,
    obs_ref, noise_ref, prior_ref, mask_ref, kappa_ref, prec_ref,
    s_mask, s_right, b_mask, b_right, down, joins, nc,
    s_z, s_one, s_two, b_z, b_one, b_two, pads, cols_out, side_in, rows_in,
    sums_y, sums_t, mine, one_row,
    send_big, recv_big, halo_send, halo_recv, sum_send, sum_recv, own_sem, in_sem,
):
    me, y = lax.axis_index("tm"), lax.axis_index("rows")
    j = patch_of(me)

    barrier = pltpu.get_barrier_semaphore()

    def each_peer(act):
        for o in FAR_FIRST:
            t = me + o
            act(t - jnp.where(t >= NT, NT, 0))

    def greet(t):
        pl.semaphore_signal(barrier, inc=1, device_id={"tm": t}, device_id_type=MESH)

    loads = [
        pltpu.make_async_copy(src, dst, in_sem.at[i])
        for i, (src, dst) in enumerate(
            (
                (mask_hbm, mask_ref),
                (obs_hbm, obs_ref),
                (noise_hbm, noise_ref),
                (prior_hbm, prior_ref),
                (prec_hbm, prec_ref),
                (kappa_hbm, kappa_ref),
            )
        )
    ]
    for load in loads:
        load.start()

    each_peer(greet)
    for k in (4, 3, 5, 2, 6, 1, 7):
        t = lax.rem(y + k, NY)
        pl.semaphore_signal(barrier, inc=1, device_id={"rows": t}, device_id_type=MESH)
    for load in loads:
        load.wait()

    for tile in range(8):
        cols = slice(128 * tile, 128 * tile + 128)
        mask = mask_ref[:, :, cols].astype(F32)
        prec = prec_ref[:, cols][None]
        right = mask * (prec * obs_ref[:, :, cols] + jnp.sqrt(prec) * noise_ref[:, :, cols])
        right = right + prior_ref[:, :, cols]
        r_all[:, :, cols] = right
        mask, right = ring_order(swap_blocks(mask), tile), ring_order(swap_blocks(right), tile)
        for h in range(2):
            at = pl.ds(16 * ring_tile(tile) + h, 8, stride=2)
            s_mask[at, :] = mask[h]
            s_right[at, :] = right[h]

    pl.semaphore_wait(barrier, NT - 1 + NY - 1)

    def to_all(src, dst, slot, rows):
        def send(t):
            pltpu.make_async_remote_copy(
                src_ref=src.at[pl.ds(rows * t, rows)],
                dst_ref=dst.at[pl.ds(rows * me, rows)],
                send_sem=send_big.at[slot],
                recv_sem=recv_big.at[slot],
                device_id={"tm": t},
                device_id_type=MESH,
            ).start()

        each_peer(send)
        own = pltpu.make_async_copy(
            src.at[pl.ds(rows * me, rows)], dst.at[pl.ds(rows * me, rows)], own_sem.at[slot]
        )
        own.start()
        return own

    def big(src, dst, slot, rows):
        n = rows * (NT - 1)
        return pltpu.make_async_remote_copy(
            src_ref=src.at[pl.ds(0, n)],
            dst_ref=dst.at[pl.ds(0, n)],
            send_sem=send_big.at[slot],
            recv_sem=recv_big.at[slot],
            device_id={"tm": lax.rem(me + 1, NT)},
            device_id_type=MESH,
        )

    own_mask = to_all(s_mask, b_mask, 0, 2)
    own_right = to_all(s_right, b_right, 1, 2)

    tile, back = j // 8, j % 8
    columns = pl.ds(pl.multiple_of(tile * 128, 128), 128)
    one_row[...] = swap_blocks(1.0 / (kappa_ref[:, columns] + 4.0))
    per_stencil = jnp.broadcast_to(one_row[pl.ds(back, 1), :], (8, 128))
    mine[...] = swap_blocks(prec_ref[:, columns])
    ratio = per_stencil * mine[pl.ds(back, 1), :]

    own_mask.wait()
    big(s_mask, b_mask, 0, 2).wait_recv()

    seg = iota((8, 128), 0)
    ones, zeros = jnp.ones((8, 128), F32), jnp.zeros((8, 128), F32)
    w = [b_mask[pl.ds(k, 8, stride=16), :] * ratio for k in range(16)]
    a, b, c, d = ones, zeros, zeros, ones
    for k in range(16):
        ac, bd = a + c, b + d
        a, b, c, d = w[k] * ac + RHO_SQ * a, w[k] * bd + RHO_SQ * b, ac, bd
    scale = 1.0 / (c + d)
    a, b, c, d = a * scale, b * scale, c * scale, d * scale
    for n in (1, 2, 4):
        pa, pb, pc, pd = [pltpu.roll(q, n, 0) for q in (a, b, c, d)]
        keep = seg < n
        a, b, c, d = [
            jnp.where(keep, old, new)
            for old, new in zip(
                (a, b, c, d),
                (a * pa + b * pc, a * pb + b * pd, c * pa + d * pc, c * pb + d * pd),
            )
        ]
    b = jnp.where(seg == 0, 0.0, pltpu.roll(b, 1, 0))
    d = jnp.where(seg == 0, 1.0, pltpu.roll(d, 1, 0))
    inverses = []
    for k in range(16):
        before_b, before_d = b, d
        bd = b + d
        b, d = w[k] * bd + RHO_SQ * b, bd
        inverse = d / (b + d)
        if k == 15:
            before = before_b / before_d
            final = w[k] + ((1.0 - RHO_SQ) + before) / (1.0 + before)
            inverse = jnp.where(seg == 7, 1.0 / final, inverse)
        inverses.append(inverse)
    carry = [RHO * inverse for inverse in inverses]
    carry[15] = jnp.where(seg == 7, 0.0, carry[15])
    into = pltpu.roll(carry[15], 1, 0)
    for k in range(16):
        down[0, k], down[1, k], down[2, k] = inverses[k], carry[k], into
        if k < 15:
            into = into * carry[k]
    back_in = carry[15]
    for k in range(15, -1, -1):
        down[3, k] = back_in
        if k > 0:
            back_in = back_in * carry[k - 1]
    for i, n in enumerate((1, 2, 4)):
        joins[i], joins[3 + i] = into, back_in
        into, back_in = into * pltpu.roll(into, n, 0), back_in * pltpu.roll(back_in, 8 - n, 0)

    def solve(load, keep):
        y, values = None, []
        for k in range(16):
            f = load(k) * per_stencil
            y = f if k == 0 else f + down[1, k - 1] * y
            values.append(y)
        for i, n in enumerate((1, 2, 4)):
            y = y + joins[i] * pltpu.roll(y, n, 0)
        y = pltpu.roll(y, 1, 0)
        values = [(v + down[2, k] * y) * down[0, k] for k, v in enumerate(values)]
        for k in range(14, -1, -1):
            values[k] = values[k] + down[1, k] * values[k + 1]
        z = values[0]
        for i, n in enumerate((1, 2, 4)):
            z = z + joins[3 + i] * pltpu.roll(z, 8 - n, 0)
        z = pltpu.roll(z, 7, 0)
        for k in range(16):
            values[k] = values[k] + down[3, k] * z
            keep(k, values[k])
        return values

    left, right_dev = device_of(lax.rem(j + NT - 1, NT)), device_of(lax.rem(j + 1, NT))
    above, below = lax.rem(y + NY - 1, NY), lax.rem(y + 1, NY)

    def halo_copies(n):
        pad = pads.at[n]
        parts = (
            (pad.at[pl.ds(8, 16)], rows_in.at[n, 1], {"rows": above}),
            (pad.at[pl.ds(32 * 7 + 8, 16)], rows_in.at[n, 0], {"rows": below}),
            (cols_out.at[n, 0], side_in.at[n, 1], {"tm": left}),
            (cols_out.at[n, 1], side_in.at[n, 0], {"tm": right_dev}),
        )
        return [
            pltpu.make_async_remote_copy(
                src_ref=src,
                dst_ref=dst,
                send_sem=halo_send.at[4 * n + i],
                recv_sem=halo_recv.at[4 * n + i],
                device_id=to,
                device_id_type=MESH,
            )
            for i, (src, dst, to) in enumerate(parts)
        ]

    def halo_start(n, v):
        for r in range(8):
            pads[n, pl.ds(32 * r + 8, 16), :] = v[16 * r : 16 * r + 16]
        cols_out[n, 0] = pads[n, pl.ds(8, 8, stride=32), :]
        cols_out[n, 1] = pads[n, pl.ds(23, 8, stride=32), :]
        copies = halo_copies(n)
        for copy in copies:
            copy.start()
        return copies

    hour = iota((16, 128), 1)
    from_before = jnp.where(hour == 0, 0.0, RHO).astype(F32)
    from_after = jnp.where(hour == 127, 0.0, RHO).astype(F32)
    weight = jnp.where((hour == 0) | (hour == 127), 1.0, 1.0 + RHO_SQ).astype(F32)

    def neighbours(n, copies):
        for copy in copies:
            copy.wait_recv()
        pads[n, pl.ds(7, 8, stride=32), :] = jnp.where(j == 0, 0.0, side_in[n, 0])
        pads[n, pl.ds(24, 8, stride=32), :] = jnp.where(j == NT - 1, 0.0, side_in[n, 1])
        for r in range(8):
            if r == 0:
                up = jnp.where(y == 0, 0.0, rows_in[n, 0])
            else:
                up = pads[n, pl.ds(32 * (r - 1) + 8, 16), :]
            if r == 7:
                down = jnp.where(y == NY - 1, 0.0, rows_in[n, 1])
            else:
                down = pads[n, pl.ds(32 * (r + 1) + 8, 16), :]
            u = pads[n, pl.ds(32 * r + 7, 16), :] + pads[n, pl.ds(32 * r + 9, 16), :]
            u = u + (up + down)
            u = weight * u - (
                from_before * pltpu.roll(u, 1, 1) + from_after * pltpu.roll(u, 127, 1)
            )
            nc[pl.ds(16 * r, 16), :] = u
        return nc[...]

    own_right.wait()
    big(s_right, b_right, 1, 2).wait_recv()
    def right_at(k):
        return b_right[pl.ds(k, 8, stride=16), :]

    def keep_z(k, v):
        s_z[pl.ds(k, 8, stride=16), :] = v

    def total_of(load, values):
        return sum(load(k) * v for k, v in enumerate(values))

    z_values = solve(right_at, keep_z)
    copies_0 = halo_start(0, s_z[...].T)
    rz_part = total_of(right_at, z_values)

    def pair(ref, n):
        ref[pl.ds(0, 128, stride=2), :] = n.T

        def load(k):
            return ref[pl.ds(2 * k, 8, stride=32), :]

        def keep(k, v):
            ref[pl.ds(2 * k + 1, 8, stride=32), :] = v

        return load, solve(load, keep)

    n0 = neighbours(0, copies_0)
    load_0, s_values = pair(s_one, n0)
    copies_1 = halo_start(1, s_one[pl.ds(1, 128, stride=2), :].T)
    own_z = to_all(s_z, b_z, 2, 2)
    own_one = to_all(s_one, b_one, 3, 4)
    e1_part = total_of(right_at, s_values)
    e2_part = total_of(load_0, s_values)

    n1 = neighbours(1, copies_1)
    e3_part = fold(n1 * jnp.concatenate([pads[1, pl.ds(32 * r + 8, 16), :] for r in range(8)], axis=0))

    sub = iota((8, 128), 0)
    total = jnp.zeros((8, 128), F32)
    for i, part in enumerate((rz_part, e1_part, e2_part, e3_part)):
        total = jnp.where(sub == i, jnp.sum(part, axis=0, keepdims=True), total)
    total = total + pltpu.roll(total, 64, 1)
    total = total + pltpu.roll(total, 32, 1)
    total = jnp.where(iota((8, 128), 1) // 32 == sub, total, 0.0)
    one_row[...] = jnp.broadcast_to(jnp.sum(total, axis=0, keepdims=True), (8, 128))
    sums_t[pl.ds(me, 1), :] = one_row[0:1, :]

    def send_sum(t):
        pltpu.make_async_remote_copy(
            src_ref=one_row.at[pl.ds(0, 1)],
            dst_ref=sums_t.at[pl.ds(me, 1)],
            send_sem=sum_send.at[1],
            recv_sem=sum_recv.at[1],
            device_id={"tm": t},
            device_id_type=MESH,
        ).start()

    each_peer(send_sum)

    pair(s_two, n1)
    own_two = to_all(s_two, b_two, 4, 4)

    def all_rows(n, src, dst, slot):
        return pltpu.make_async_remote_copy(
            src_ref=src.at[pl.ds(0, n)],
            dst_ref=dst.at[pl.ds(0, n)],
            send_sem=sum_send.at[slot],
            recv_sem=sum_recv.at[slot],
            device_id={"rows": lax.rem(y + 1, NY)},
            device_id_type=MESH,
        )

    all_rows(NT - 1, sums_t, sums_t, 1).wait_recv()
    mine[...] = fold(sums_t[...])
    sums_y[pl.ds(pl.multiple_of(8 * y, 8), 8), :] = mine[...]
    for k in (4, 3, 5, 2, 6, 1, 7):
        pltpu.make_async_remote_copy(
            src_ref=mine,
            dst_ref=sums_y.at[pl.ds(pl.multiple_of(8 * y, 8), 8)],
            send_sem=sum_send.at[0],
            recv_sem=sum_recv.at[0],
            device_id={"rows": lax.rem(y + k, NY)},
            device_id_type=MESH,
        ).start()

    outs = (
        (0, b_z, 2, 0, z_all),
        (1, b_one, 4, 0, na_all),
        (2, b_one, 4, 1, sa_all),
        (3, b_two, 4, 0, nb_all),
        (4, b_two, 4, 1, sb_all),
    )
    for i, ref, stride, o, dst in outs:
        if i == 0:
            own_z.wait()
            big(s_z, b_z, 2, 2).wait_recv()
        elif i == 1:
            own_one.wait()
            big(s_one, b_one, 3, 4).wait_recv()
        elif i == 3:
            own_two.wait()
            big(s_two, b_two, 4, 4).wait_recv()
        for tile in range(8):
            for h in range(2):
                at = pl.ds(8 * stride * ring_tile(tile) + h * (stride // 2) + o, 8, stride=stride)
                dst[h, :, 128 * tile : 128 * tile + 128] = swap_blocks(ring_order(ref[at, :], tile))

    all_rows(8 * (NY - 1), sums_y, sums_y, 0).wait_recv()
    sums = jnp.sum(fold(sums_y[...]), axis=0, keepdims=True)
    group = iota((1, 128), 1) // 32
    rz0, e1, e2, e3 = [lane_sum(jnp.where(group == i, sums, 0.0)) for i in range(4)]
    curved = rz0 - e1
    alpha0 = rz0 / curved
    beta0 = (e2 * rz0 - e1 * e1) / (curved * curved)
    along = 1.0 + beta0 - alpha0
    curved1 = along * along * curved + 2.0 * along * alpha0 * (e1 - e2) + alpha0 * alpha0 * (e2 - e3)
    alpha1 = beta0 * rz0 / curved1
    first = alpha0 + alpha1 * (1.0 + beta0)
    second = alpha0 * alpha1
    c0, c1 = 1.0 - first + second, first - 2.0 * second

    row = iota((8, 128), 0)
    coef_ref[...] = jnp.where(
        row == 0,
        first - second,
        jnp.where(row == 1, second, jnp.where(row == 2, c0, c1)),
    )
    for copy in copies_0 + copies_1:
        copy.wait_send()
    big(s_mask, b_mask, 0, 2).wait_send()
    big(s_right, b_right, 1, 2).wait_send()
    big(s_z, b_z, 2, 2).wait_send()
    big(s_one, b_one, 3, 4).wait_send()
    big(s_two, b_two, 4, 4).wait_send()
    all_rows(8 * (NY - 1), sums_y, sums_y, 0).wait_send()
    all_rows(NT - 1, sums_t, sums_t, 1).wait_send()


def combine(z_ref, na_ref, sa_ref, nb_ref, sb_ref, r_ref, coef_ref, x_out, r_out, p_out):
    q0, q1, q2, q3 = [coef_ref[i : i + 1, 0:1].reshape(1, 1, 1) for i in range(4)]
    for tile in range(8):
        at = (slice(None), slice(None), slice(128 * tile, 128 * tile + 128))
        z, sa = z_ref[at], sa_ref[at]
        x_out[at] = q0 * z + q1 * sa
        r_out[at] = q2 * r_ref[at] + q3 * na_ref[at] + q1 * nb_ref[at]
        p_out[at] = q2 * z + q3 * sa + q1 * sb_ref[at]


def per_device(observations, obs_noise, prior_noise, observed, kappa_sq, obs_precision):
    vmem = pl.BlockSpec(memory_space=pltpu.VMEM)
    hbm = pl.BlockSpec(memory_space=pl.ANY)
    out = jax.ShapeDtypeStruct(observations.shape, F32)

    def buf(*shape):
        return pltpu.VMEM(shape, F32)

    block = observations.shape
    parts = pl.pallas_call(
        kernel,
        out_shape=(buf(*block),) * 6 + (buf(8, 128),),
        in_specs=[hbm] * 6,
        out_specs=(vmem,) * 7,
        scratch_shapes=[
            buf(*block), buf(*block), buf(*block), pltpu.VMEM(block, jnp.int32),
            buf(*kappa_sq.shape), buf(*kappa_sq.shape),
            buf(128, 128), buf(128, 128), buf(128, 128), buf(128, 128),
            buf(4, 16, 8, 128), buf(6, 8, 128), buf(128, 128),
            buf(128, 128), buf(256, 128), buf(256, 128),
            buf(128, 128), buf(256, 128), buf(256, 128),
            buf(2, 256, 128), buf(2, 2, 8, 128), buf(2, 2, 8, 128), buf(2, 2, 16, 128),
            buf(64, 128), buf(64, 128), buf(8, 128), buf(8, 128),
            pltpu.SemaphoreType.DMA((5,)), pltpu.SemaphoreType.DMA((5,)),
            pltpu.SemaphoreType.DMA((8,)), pltpu.SemaphoreType.DMA((8,)),
            pltpu.SemaphoreType.DMA((2,)), pltpu.SemaphoreType.DMA((2,)),
            pltpu.SemaphoreType.DMA((5,)), pltpu.SemaphoreType.DMA((6,)),
        ],
        compiler_params=pltpu.CompilerParams(collective_id=0, has_side_effects=True),
    )(observations, obs_noise, prior_noise, observed, kappa_sq, obs_precision)
    return pl.pallas_call(
        combine, out_shape=(out, out, out), in_specs=[vmem] * 7, out_specs=(vmem,) * 3
    )(*[pltpu.with_memory_space_constraint(part, pltpu.VMEM) for part in parts])


def solution(mesh):
    in_specs = (P("tm", "rows", None),) * 4 + (P("rows", None),) * 2
    out_specs = (P("tm", "rows", None),) * 3
    return jax.shard_map(
        per_device, mesh=mesh, in_specs=in_specs, out_specs=out_specs, check_vma=False
    )
```

```python
import jax
import jax.numpy as jnp
from jax import lax
from jax.experimental import pallas as pl
from jax.experimental.pallas import tpu as pltpu
from jax.sharding import PartitionSpec as P

RHO = 0.995
RHO_SQ = RHO * RHO
MESH = pl.DeviceIdType.MESH
F32 = jnp.float32
NT = 64
NY = 8


def hops(o):
    z, x = (o // 2) % 8, o // 16
    return min(z, 8 - z) + min(x, 4 - x)


FAR_FIRST = sorted(range(1, NT), key=lambda o: (-hops(o), o))


def patch_of(m):
    x, z, c = m // 16, (m // 2) % 8, m % 2
    odd = x % 2
    return 16 * x + 2 * (z + odd * (7 - 2 * z)) + c


def device_of(j):
    return patch_of(j)


def ring_tile(tile):
    return tile + (0, 0, 1, -1)[tile % 4]


def ring_order(v, tile):
    if tile % 4 < 2:
        return v
    axis = v.ndim - 2
    v = pltpu.roll(v, 4, axis)
    even = (iota(v.shape, axis) // 2) % 2 == 0
    return jnp.where(even, pltpu.roll(v, 6, axis), pltpu.roll(v, 2, axis))


def iota(shape, axis):
    return lax.broadcasted_iota(jnp.int32, shape, axis)


def swap_blocks(v):
    shape, sub, lane = v.shape, v.ndim - 2, v.ndim - 1
    s, g = iota(shape, sub), iota(shape, lane) // 16
    for b in (1, 2, 4):
        down = pltpu.roll(pltpu.roll(v, 8 - b, sub), 16 * b, lane)
        s_b, g_b = (s // b) % 2, (g // b) % 2
        if b == 4:
            v = jnp.where(s_b == g_b, v, down)
        else:
            up = pltpu.roll(pltpu.roll(v, b, sub), 128 - 16 * b, lane)
            v = jnp.where(s_b == g_b, v, jnp.where(s_b == 0, down, up))
    return v


def lane_sum(v):
    return jnp.sum(v, axis=1, keepdims=True)


def fold(v):
    return jnp.sum(v.reshape(v.shape[0] // 8, 8, 128), axis=0)


def kernel(
    obs_hbm, noise_hbm, prior_hbm, mask_hbm, kappa_hbm, prec_hbm,
    z_all, na_all, sa_all, nb_all, sb_all, r_all, coef_ref,
    obs_ref, noise_ref, prior_ref, mask_ref, kappa_ref, prec_ref,
    s_mask, s_right, b_mask, b_right, down, joins, nc,
    s_z, s_one, s_two, b_z, b_one, b_two, pads, cols_out, side_in, rows_in,
    sums_y, sums_t, mine, one_row,
    send_big, recv_big, halo_send, halo_recv, sum_send, sum_recv, own_sem, in_sem,
):
    me, y = lax.axis_index("tm"), lax.axis_index("rows")
    j = patch_of(me)

    barrier = pltpu.get_barrier_semaphore()

    def each_peer(act):
        for o in FAR_FIRST:
            t = me + o
            act(t - jnp.where(t >= NT, NT, 0))

    def greet(t):
        pl.semaphore_signal(barrier, inc=1, device_id={"tm": t}, device_id_type=MESH)

    loads = [
        pltpu.make_async_copy(src, dst, in_sem.at[i])
        for i, (src, dst) in enumerate(
            (
                (mask_hbm, mask_ref),
                (obs_hbm, obs_ref),
                (noise_hbm, noise_ref),
                (prior_hbm, prior_ref),
                (prec_hbm, prec_ref),
                (kappa_hbm, kappa_ref),
            )
        )
    ]
    for load in loads:
        load.start()

    each_peer(greet)
    for k in (4, 3, 5, 2, 6, 1, 7):
        t = lax.rem(y + k, NY)
        pl.semaphore_signal(barrier, inc=1, device_id={"rows": t}, device_id_type=MESH)
    for load in loads:
        load.wait()

    for tile in range(8):
        cols = slice(128 * tile, 128 * tile + 128)
        mask = mask_ref[:, :, cols].astype(F32)
        prec = prec_ref[:, cols][None]
        right = mask * (prec * obs_ref[:, :, cols] + jnp.sqrt(prec) * noise_ref[:, :, cols])
        right = right + prior_ref[:, :, cols]
        r_all[:, :, cols] = right
        mask, right = ring_order(swap_blocks(mask), tile), ring_order(swap_blocks(right), tile)
        for h in range(2):
            at = pl.ds(16 * ring_tile(tile) + h, 8, stride=2)
            s_mask[at, :] = mask[h]
            s_right[at, :] = right[h]

    pl.semaphore_wait(barrier, NT - 1 + NY - 1)

    def to_all(src, dst, slot, rows):
        def send(t):
            pltpu.make_async_remote_copy(
                src_ref=src.at[pl.ds(rows * t, rows)],
                dst_ref=dst.at[pl.ds(rows * me, rows)],
                send_sem=send_big.at[slot],
                recv_sem=recv_big.at[slot],
                device_id={"tm": t},
                device_id_type=MESH,
            ).start()

        each_peer(send)
        own = pltpu.make_async_copy(
            src.at[pl.ds(rows * me, rows)], dst.at[pl.ds(rows * me, rows)], own_sem.at[slot]
        )
        own.start()
        return own

    def big(src, dst, slot, rows):
        n = rows * (NT - 1)
        return pltpu.make_async_remote_copy(
            src_ref=src.at[pl.ds(0, n)],
            dst_ref=dst.at[pl.ds(0, n)],
            send_sem=send_big.at[slot],
            recv_sem=recv_big.at[slot],
            device_id={"tm": lax.rem(me + 1, NT)},
            device_id_type=MESH,
        )

    own_mask = to_all(s_mask, b_mask, 0, 2)
    own_right = to_all(s_right, b_right, 1, 2)

    tile, back = j // 8, j % 8
    columns = pl.ds(pl.multiple_of(tile * 128, 128), 128)
    one_row[...] = swap_blocks(1.0 / (kappa_ref[:, columns] + 4.0))
    per_stencil = jnp.broadcast_to(one_row[pl.ds(back, 1), :], (8, 128))
    mine[...] = swap_blocks(prec_ref[:, columns])
    ratio = per_stencil * mine[pl.ds(back, 1), :]

    own_mask.wait()
    big(s_mask, b_mask, 0, 2).wait_recv()

    seg = iota((8, 128), 0)
    ones, zeros = jnp.ones((8, 128), F32), jnp.zeros((8, 128), F32)
    w = [b_mask[pl.ds(k, 8, stride=16), :] * ratio for k in range(16)]
    a, b, c, d = ones, zeros, zeros, ones
    for k in range(16):
        ac, bd = a + c, b + d
        a, b, c, d = w[k] * ac + RHO_SQ * a, w[k] * bd + RHO_SQ * b, ac, bd
    scale = 1.0 / (c + d)
    a, b, c, d = a * scale, b * scale, c * scale, d * scale
    for n in (1, 2, 4):
        pa, pb, pc, pd = [pltpu.roll(q, n, 0) for q in (a, b, c, d)]
        keep = seg < n
        a, b, c, d = [
            jnp.where(keep, old, new)
            for old, new in zip(
                (a, b, c, d),
                (a * pa + b * pc, a * pb + b * pd, c * pa + d * pc, c * pb + d * pd),
            )
        ]
    b = jnp.where(seg == 0, 0.0, pltpu.roll(b, 1, 0))
    d = jnp.where(seg == 0, 1.0, pltpu.roll(d, 1, 0))
    inverses = []
    for k in range(16):
        before_b, before_d = b, d
        bd = b + d
        b, d = w[k] * bd + RHO_SQ * b, bd
        inverse = d / (b + d)
        if k == 15:
            before = before_b / before_d
            final = w[k] + ((1.0 - RHO_SQ) + before) / (1.0 + before)
            inverse = jnp.where(seg == 7, 1.0 / final, inverse)
        inverses.append(inverse)
    carry = [RHO * inverse for inverse in inverses]
    carry[15] = jnp.where(seg == 7, 0.0, carry[15])
    into = pltpu.roll(carry[15], 1, 0)
    for k in range(16):
        down[0, k], down[1, k], down[2, k] = inverses[k], carry[k], into
        if k < 15:
            into = into * carry[k]
    back_in = carry[15]
    for k in range(15, -1, -1):
        down[3, k] = back_in
        if k > 0:
            back_in = back_in * carry[k - 1]
    for i, n in enumerate((1, 2, 4)):
        joins[i], joins[3 + i] = into, back_in
        into, back_in = into * pltpu.roll(into, n, 0), back_in * pltpu.roll(back_in, 8 - n, 0)

    def solve(load, keep):
        y, values = None, []
        for k in range(16):
            f = load(k) * per_stencil
            y = f if k == 0 else f + down[1, k - 1] * y
            values.append(y)
        for i, n in enumerate((1, 2, 4)):
            y = y + joins[i] * pltpu.roll(y, n, 0)
        y = pltpu.roll(y, 1, 0)
        values = [(v + down[2, k] * y) * down[0, k] for k, v in enumerate(values)]
        for k in range(14, -1, -1):
            values[k] = values[k] + down[1, k] * values[k + 1]
        z = values[0]
        for i, n in enumerate((1, 2, 4)):
            z = z + joins[3 + i] * pltpu.roll(z, 8 - n, 0)
        z = pltpu.roll(z, 7, 0)
        for k in range(16):
            values[k] = values[k] + down[3, k] * z
            keep(k, values[k])
        return values

    left, right_dev = device_of(lax.rem(j + NT - 1, NT)), device_of(lax.rem(j + 1, NT))
    above, below = lax.rem(y + NY - 1, NY), lax.rem(y + 1, NY)

    def halo_copies(n):
        pad = pads.at[n]
        parts = (
            (pad.at[pl.ds(8, 16)], rows_in.at[n, 1], {"rows": above}),
            (pad.at[pl.ds(32 * 7 + 8, 16)], rows_in.at[n, 0], {"rows": below}),
            (cols_out.at[n, 0], side_in.at[n, 1], {"tm": left}),
            (cols_out.at[n, 1], side_in.at[n, 0], {"tm": right_dev}),
        )
        return [
            pltpu.make_async_remote_copy(
                src_ref=src,
                dst_ref=dst,
                send_sem=halo_send.at[4 * n + i],
                recv_sem=halo_recv.at[4 * n + i],
                device_id=to,
                device_id_type=MESH,
            )
            for i, (src, dst, to) in enumerate(parts)
        ]

    def halo_start(n, v):
        for r in range(8):
            pads[n, pl.ds(32 * r + 8, 16), :] = v[16 * r : 16 * r + 16]
        cols_out[n, 0] = pads[n, pl.ds(8, 8, stride=32), :]
        cols_out[n, 1] = pads[n, pl.ds(23, 8, stride=32), :]
        copies = halo_copies(n)
        for copy in copies:
            copy.start()
        return copies

    hour = iota((16, 128), 1)
    from_before = jnp.where(hour == 0, 0.0, RHO).astype(F32)
    from_after = jnp.where(hour == 127, 0.0, RHO).astype(F32)
    weight = jnp.where((hour == 0) | (hour == 127), 1.0, 1.0 + RHO_SQ).astype(F32)

    def neighbours(n, copies):
        for copy in copies:
            copy.wait_recv()
        pads[n, pl.ds(7, 8, stride=32), :] = jnp.where(j == 0, 0.0, side_in[n, 0])
        pads[n, pl.ds(24, 8, stride=32), :] = jnp.where(j == NT - 1, 0.0, side_in[n, 1])
        for r in range(8):
            if r == 0:
                up = jnp.where(y == 0, 0.0, rows_in[n, 0])
            else:
                up = pads[n, pl.ds(32 * (r - 1) + 8, 16), :]
            if r == 7:
                down = jnp.where(y == NY - 1, 0.0, rows_in[n, 1])
            else:
                down = pads[n, pl.ds(32 * (r + 1) + 8, 16), :]
            u = pads[n, pl.ds(32 * r + 7, 16), :] + pads[n, pl.ds(32 * r + 9, 16), :]
            u = u + (up + down)
            u = weight * u - (
                from_before * pltpu.roll(u, 1, 1) + from_after * pltpu.roll(u, 127, 1)
            )
            nc[pl.ds(16 * r, 16), :] = u
        return nc[...]

    own_right.wait()
    big(s_right, b_right, 1, 2).wait_recv()
    def right_at(k):
        return b_right[pl.ds(k, 8, stride=16), :]

    def keep_z(k, v):
        s_z[pl.ds(k, 8, stride=16), :] = v

    def total_of(load, values):
        return sum(load(k) * v for k, v in enumerate(values))

    z_values = solve(right_at, keep_z)
    copies_0 = halo_start(0, s_z[...].T)
    rz_part = total_of(right_at, z_values)
    own_z = to_all(s_z, b_z, 2, 2)

    def pair(ref, n):
        ref[pl.ds(0, 128, stride=2), :] = n.T

        def load(k):
            return ref[pl.ds(2 * k, 8, stride=32), :]

        def keep(k, v):
            ref[pl.ds(2 * k + 1, 8, stride=32), :] = v

        return load, solve(load, keep)

    n0 = neighbours(0, copies_0)
    load_0, s_values = pair(s_one, n0)
    copies_1 = halo_start(1, s_one[pl.ds(1, 128, stride=2), :].T)
    own_one = to_all(s_one, b_one, 3, 4)
    e1_part = total_of(right_at, s_values)
    e2_part = total_of(load_0, s_values)

    n1 = neighbours(1, copies_1)
    e3_part = fold(n1 * jnp.concatenate([pads[1, pl.ds(32 * r + 8, 16), :] for r in range(8)], axis=0))

    sub = iota((8, 128), 0)
    total = jnp.zeros((8, 128), F32)
    for i, part in enumerate((rz_part, e1_part, e2_part, e3_part)):
        total = jnp.where(sub == i, jnp.sum(part, axis=0, keepdims=True), total)
    total = total + pltpu.roll(total, 64, 1)
    total = total + pltpu.roll(total, 32, 1)
    total = jnp.where(iota((8, 128), 1) // 32 == sub, total, 0.0)
    one_row[...] = jnp.broadcast_to(jnp.sum(total, axis=0, keepdims=True), (8, 128))
    sums_t[pl.ds(me, 1), :] = one_row[0:1, :]

    def send_sum(t):
        pltpu.make_async_remote_copy(
            src_ref=one_row.at[pl.ds(0, 1)],
            dst_ref=sums_t.at[pl.ds(me, 1)],
            send_sem=sum_send.at[1],
            recv_sem=sum_recv.at[1],
            device_id={"tm": t},
            device_id_type=MESH,
        ).start()

    each_peer(send_sum)

    pair(s_two, n1)
    own_two = to_all(s_two, b_two, 4, 4)

    def all_rows(n, src, dst, slot):
        return pltpu.make_async_remote_copy(
            src_ref=src.at[pl.ds(0, n)],
            dst_ref=dst.at[pl.ds(0, n)],
            send_sem=sum_send.at[slot],
            recv_sem=sum_recv.at[slot],
            device_id={"rows": lax.rem(y + 1, NY)},
            device_id_type=MESH,
        )

    all_rows(NT - 1, sums_t, sums_t, 1).wait_recv()
    mine[...] = fold(sums_t[...])
    sums_y[pl.ds(pl.multiple_of(8 * y, 8), 8), :] = mine[...]
    for k in (4, 3, 5, 2, 6, 1, 7):
        pltpu.make_async_remote_copy(
            src_ref=mine,
            dst_ref=sums_y.at[pl.ds(pl.multiple_of(8 * y, 8), 8)],
            send_sem=sum_send.at[0],
            recv_sem=sum_recv.at[0],
            device_id={"rows": lax.rem(y + k, NY)},
            device_id_type=MESH,
        ).start()

    outs = (
        (0, b_z, 2, 0, z_all),
        (1, b_one, 4, 0, na_all),
        (2, b_one, 4, 1, sa_all),
        (3, b_two, 4, 0, nb_all),
        (4, b_two, 4, 1, sb_all),
    )
    for i, ref, stride, o, dst in outs:
        if i == 0:
            own_z.wait()
            big(s_z, b_z, 2, 2).wait_recv()
        elif i == 1:
            own_one.wait()
            big(s_one, b_one, 3, 4).wait_recv()
        elif i == 3:
            own_two.wait()
            big(s_two, b_two, 4, 4).wait_recv()
        for tile in range(8):
            for h in range(2):
                at = pl.ds(8 * stride * ring_tile(tile) + h * (stride // 2) + o, 8, stride=stride)
                dst[h, :, 128 * tile : 128 * tile + 128] = swap_blocks(ring_order(ref[at, :], tile))

    all_rows(8 * (NY - 1), sums_y, sums_y, 0).wait_recv()
    sums = jnp.sum(fold(sums_y[...]), axis=0, keepdims=True)
    group = iota((1, 128), 1) // 32
    rz0, e1, e2, e3 = [lane_sum(jnp.where(group == i, sums, 0.0)) for i in range(4)]
    curved = rz0 - e1
    alpha0 = rz0 / curved
    beta0 = (e2 * rz0 - e1 * e1) / (curved * curved)
    along = 1.0 + beta0 - alpha0
    curved1 = along * along * curved + 2.0 * along * alpha0 * (e1 - e2) + alpha0 * alpha0 * (e2 - e3)
    alpha1 = beta0 * rz0 / curved1
    first = alpha0 + alpha1 * (1.0 + beta0)
    second = alpha0 * alpha1
    c0, c1 = 1.0 - first + second, first - 2.0 * second

    row = iota((8, 128), 0)
    coef_ref[...] = jnp.where(
        row == 0,
        first - second,
        jnp.where(row == 1, second, jnp.where(row == 2, c0, c1)),
    )
    for copy in copies_0 + copies_1:
        copy.wait_send()
    big(s_mask, b_mask, 0, 2).wait_send()
    big(s_right, b_right, 1, 2).wait_send()
    big(s_z, b_z, 2, 2).wait_send()
    big(s_one, b_one, 3, 4).wait_send()
    big(s_two, b_two, 4, 4).wait_send()
    all_rows(8 * (NY - 1), sums_y, sums_y, 0).wait_send()
    all_rows(NT - 1, sums_t, sums_t, 1).wait_send()


def combine(z_ref, na_ref, sa_ref, nb_ref, sb_ref, r_ref, coef_ref, x_out, r_out, p_out):
    q0, q1, q2, q3 = [coef_ref[i : i + 1, 0:1].reshape(1, 1, 1) for i in range(4)]
    for tile in range(8):
        at = (slice(None), slice(None), slice(128 * tile, 128 * tile + 128))
        z, sa = z_ref[at], sa_ref[at]
        x_out[at] = q0 * z + q1 * sa
        r_out[at] = q2 * r_ref[at] + q3 * na_ref[at] + q1 * nb_ref[at]
        p_out[at] = q2 * z + q3 * sa + q1 * sb_ref[at]


def per_device(observations, obs_noise, prior_noise, observed, kappa_sq, obs_precision):
    vmem = pl.BlockSpec(memory_space=pltpu.VMEM)
    hbm = pl.BlockSpec(memory_space=pl.ANY)
    out = jax.ShapeDtypeStruct(observations.shape, F32)

    def buf(*shape):
        return pltpu.VMEM(shape, F32)

    block = observations.shape
    parts = pl.pallas_call(
        kernel,
        out_shape=(buf(*block),) * 6 + (buf(8, 128),),
        in_specs=[hbm] * 6,
        out_specs=(vmem,) * 7,
        scratch_shapes=[
            buf(*block), buf(*block), buf(*block), pltpu.VMEM(block, jnp.int32),
            buf(*kappa_sq.shape), buf(*kappa_sq.shape),
            buf(128, 128), buf(128, 128), buf(128, 128), buf(128, 128),
            buf(4, 16, 8, 128), buf(6, 8, 128), buf(128, 128),
            buf(128, 128), buf(256, 128), buf(256, 128),
            buf(128, 128), buf(256, 128), buf(256, 128),
            buf(2, 256, 128), buf(2, 2, 8, 128), buf(2, 2, 8, 128), buf(2, 2, 16, 128),
            buf(64, 128), buf(64, 128), buf(8, 128), buf(8, 128),
            pltpu.SemaphoreType.DMA((5,)), pltpu.SemaphoreType.DMA((5,)),
            pltpu.SemaphoreType.DMA((8,)), pltpu.SemaphoreType.DMA((8,)),
            pltpu.SemaphoreType.DMA((2,)), pltpu.SemaphoreType.DMA((2,)),
            pltpu.SemaphoreType.DMA((5,)), pltpu.SemaphoreType.DMA((6,)),
        ],
        compiler_params=pltpu.CompilerParams(collective_id=0, has_side_effects=True),
    )(observations, obs_noise, prior_noise, observed, kappa_sq, obs_precision)
    return pl.pallas_call(
        combine, out_shape=(out, out, out), in_specs=[vmem] * 7, out_specs=(vmem,) * 3
    )(*[pltpu.with_memory_space_constraint(part, pltpu.VMEM) for part in parts])


def solution(mesh):
    in_specs = (P("tm", "rows", None),) * 4 + (P("rows", None),) * 2
    out_specs = (P("tm", "rows", None),) * 3
    return jax.shard_map(
        per_device, mesh=mesh, in_specs=in_specs, out_specs=out_specs, check_vma=False
    )
```
